32 devices in a mesh: groups: 2 (over y), sample: 4 (over x, core), space: 4 (over z).
Axes of the slice: x: 2, y: 2, z: 4, core: 2. Of those that a mesh axis runs over, the one named last changes fastest.
Arguments:
- adjoint_source: float32 [8, 56, 4, 8, 128], P(('groups', 'sample'), None, 'space'), parts along dimension 0, may hold values from -64 to 64
- kl_bank: float32 [6, 6, 4, 8, 128], P(None, None, 'space'), may hold values from -0.12 to 6, as said below
- multi_index: int32 [56, 5], replicated, may hold values from 0 to 3, as said below
- sample_ids: int32 [8], P(('groups', 'sample')), parts along dimension 0, may hold values from 0 to 5
Outputs:
- adjoint_state: float32 [8, 56, 4, 8, 128], P(('groups', 'sample'), None, 'space'), parts along dimension 0
- control_gradient: float32 [8, 8, 128], P(('groups', 'space'), 'sample'), parts along dimension 0
The draws below stay inside these ranges and needn't reach their ends.
There are 2 independent parts, one for each index of `groups`. The reference program is written for one: setup_inputs(seed, part) draws one part's arguments, and reference() takes and returns one part's arrays. A program takes and returns all parts, laid end to end along the dimension named above; an argument that names none is the same for every part. Nothing has to cross between parts.
Inputs may be any that keep to these rules, and one draw needn't show every extreme that they name: `kl_bank`: field 0 of every geometry is 2 or more; fields 1 to 5 lie between -0.12 and 0.12. `multi_index`: the rows are the 56 distinct lists of 5 degrees whose total is at most 3, each once, in some order.
All inputs are finite; a program needn't handle non-finite values.
Results may differ from the reference program's by a relative error of at most 0.00025.
Values sent between devices are 32-bit elements; how exact they have to be, the bound alone decides.
A program may use at most 64 MiB of HBM per device.

```python
import math
from functools import reduce
import jax
import jax.numpy as jnp
import numpy as np
from jax import lax

P_SIZE = 56
KL = 5
DEGREE = 3
ITERS = 2
BANK = 6
GY = 8
GZ = 128
GX = 4
SAMPLES = 4


def basis_rows():
    entries = [[]]
    for variable in range(KL):
        entries = [prefix + [height] for prefix in entries for height in range(DEGREE + 1) if sum(prefix) + height <= DEGREE]
    return np.array(entries, dtype=np.int32)


def draw_multi_index(key, part):
    basis_table = jnp.asarray(basis_rows(), jnp.int32)
    shuffle = jax.random.permutation(key, basis_table.shape[0])
    return basis_table[shuffle]


def draw_kl_bank(key, part):
    key_mean = jax.random.fold_in(key, 11)
    key_rest = jax.random.fold_in(key, 12)
    uniform_mean = jax.random.uniform(key_mean, (BANK, 1, GX, GY, GZ), jnp.float32)
    exponent = uniform_mean
    mean_field = 2.0 * jnp.exp(exponent * math.log(3.0))
    spread_rest = jax.random.uniform(key_rest, (BANK, KL, GX, GY, GZ), jnp.float32, -1.0, 1.0)
    return jnp.concatenate([mean_field, 0.12 * spread_rest], axis=1)


def draw_adjoint_source(key, part):
    key_value = jax.random.fold_in(key, 21)
    key_rows = jax.random.fold_in(key, 22)
    full_shape = (SAMPLES, P_SIZE, GX, GY, GZ)
    first_pos = lax.broadcasted_iota(jnp.float32, full_shape, 2) / max(GX - 1, 1)
    last_pos = lax.broadcasted_iota(jnp.float32, full_shape, 4) / max(GZ - 1, 1)
    row_scale = jnp.exp(math.log(10.0) * (jax.random.uniform(key_rows, (SAMPLES, 1, GX, GY, 1), jnp.float32) - 0.5))
    values = jnp.clip(jax.random.normal(key_value, full_shape, jnp.float32), -4.0, 4.0)
    rising = jnp.exp(math.log(3.0) * (first_pos + last_pos - 1.0))
    return values * row_scale * rising


def with_ends(result, rng, least, top_value):
    longest = result.shape.index(max(result.shape))
    spots = []
    for shift in (0, 1):
        where = [jax.random.randint(jax.random.fold_in(rng, axis), (), 0, length) for axis, length in enumerate(result.shape)]
        where[longest] = (where[longest] + shift) % result.shape[longest]
        spots.append(tuple(where))
    return result.at[spots[0]].set(least).at[spots[1]].set(top_value)


def setup_inputs(seed: int = 0, part: int = 0) -> dict:
    streams_of = jax.random.split(jax.random.key(seed), 5)
    part_keys = jax.random.split(jax.random.fold_in(streams_of[4], part), 5)
    return {
        "adjoint_source": draw_adjoint_source(jax.random.fold_in(jax.random.fold_in(streams_of[4], part), 71), part),
        "kl_bank": draw_kl_bank(jax.random.fold_in(streams_of[4], 71), part),
        "multi_index": draw_multi_index(jax.random.fold_in(streams_of[4], 71), part),
        "sample_ids": with_ends(jax.random.randint(part_keys[3], (SAMPLES,), 0, BANK), jax.random.fold_in(part_keys[3], 1), 0, BANK - 1).astype(jnp.int32),
    }


cross_weight = 1.0 / 64.0

def coupling_tables(multi_index):
    upper_rows = multi_index[:, None, :]
    lower_rows = multi_index[None, :, :]
    offset = upper_rows - lower_rows
    distance = lax.optimization_barrier(jnp.sum(jnp.abs(offset), axis=2))
    larger = jnp.maximum(upper_rows, lower_rows).astype(jnp.float32)
    adjacent = (jnp.abs(offset) == 1) & (distance == 1)[:, :, None]
    raising = jnp.where(adjacent, jnp.sqrt(larger), jnp.zeros_like(larger))
    identity = (distance == 0).astype(jnp.float32)
    coupling = jnp.concatenate([identity[None], jnp.transpose(raising, (2, 0, 1))], axis=0)
    mean_pick = (lax.optimization_barrier(jnp.sum(multi_index, axis=1)) == 0).astype(jnp.float32)
    return (coupling, mean_pick)

def neighbour_views(padded):
    return [padded[:, :, 2:, 1:-1, 1:-1], padded[:, :, :-2, 1:-1, 1:-1], padded[:, :, 1:-1, 2:, 1:-1], padded[:, :, 1:-1, :-2, 1:-1], padded[:, :, 1:-1, 1:-1, 2:], padded[:, :, 1:-1, 1:-1, :-2]]

def face_list(fields, padded):
    weights = [1.0, 1.0, cross_weight, cross_weight, cross_weight, cross_weight]
    return [weight * 0.5 * (fields + beside) for weight, beside in zip(weights, neighbour_views(padded))]

def line_prepare(main_band, sub_band, super_band):
    position = lax.broadcasted_iota(jnp.int32, main_band.shape, 1)
    sub_band = jnp.where(position == 0, jnp.zeros_like(sub_band), sub_band)
    super_band = jnp.where(position == main_band.shape[1] - 1, jnp.zeros_like(super_band), super_band)
    return tuple((jnp.moveaxis(band_arr, 1, 3) for band_arr in (sub_band, main_band, super_band)))

def line_bands(face_coefs):
    main_band = reduce(jnp.add, [coef[:, 0] for coef in face_coefs])
    return line_prepare(main_band, -face_coefs[1][:, 0], -face_coefs[0][:, 0])

def line_solve(residual, prepared):
    sub_band, main_band, super_band = prepared
    stacked = jnp.transpose(residual, (0, 3, 4, 2, 1))
    solved = lax.linalg.tridiagonal_solve(sub_band, main_band, super_band, stacked)
    return jnp.transpose(solved, (0, 4, 3, 1, 2))

def operate(field_in, face_coefs, coupling):
    padded = jnp.pad(field_in, ((0, 0), (0, 0), (1, 1), (1, 1), (1, 1)))
    differences = [field_in - beside for beside in neighbour_views(padded)]
    summed = jnp.zeros_like(field_in)
    for term_index in range(coupling.shape[0]):
        weighted = reduce(jnp.add, [coef[:, term_index][:, None] * change for coef, change in zip(face_coefs, differences)])
        summed = summed + jnp.einsum('ij,sjxyz->sixyz', coupling[term_index].astype(jnp.float32), weighted.astype(jnp.float32), precision=lax.Precision.HIGHEST, preferred_element_type=jnp.float32)
    return summed

def spread(values):
    return values[:, None, None, None, None]

def solve_sample(right_side, face_coefs, coupling, prepared):
    solution = jnp.zeros_like(right_side)
    residual = right_side
    smoothed = line_solve(residual, prepared)
    direction = smoothed
    fit_now = lax.optimization_barrier(jnp.sum(residual * smoothed, axis=(1, 2, 3, 4)))
    for iteration in range(ITERS):
        image_vec = operate(direction, face_coefs, coupling)
        step_size = fit_now / lax.optimization_barrier(jnp.sum(direction * image_vec, axis=(1, 2, 3, 4)))
        solution = solution + spread(step_size) * direction
        residual = residual - spread(step_size) * image_vec
        if iteration + 1 < ITERS:
            smoothed = line_solve(residual, prepared)
            fit_next = lax.optimization_barrier(jnp.sum(residual * smoothed, axis=(1, 2, 3, 4)))
            direction = smoothed + spread(fit_next / fit_now) * direction
            fit_now = fit_next
    return solution

def reference(adjoint_source, kl_bank, multi_index, sample_ids):
    coupling, mean_pick = coupling_tables(multi_index)
    solutions = []
    for sample in range(SAMPLES):
        fields = jnp.take(kl_bank, sample_ids[sample:sample + 1], axis=0)
        padded = jnp.pad(fields, ((0, 0), (0, 0), (1, 1), (1, 1), (1, 1)))
        face_coefs = face_list(fields, padded)
        prepared = line_bands(face_coefs)
        right_side = adjoint_source[sample:sample + 1]
        solutions.append(solve_sample(right_side, face_coefs, coupling, prepared))
    adjoint_state = jnp.concatenate(solutions, axis=0)
    gradient = jnp.einsum('p,spxyz->xyz', mean_pick.astype(jnp.float32), adjoint_state.astype(jnp.float32), precision=lax.Precision.HIGHEST, preferred_element_type=jnp.float32) / SAMPLES
    return (adjoint_state, gradient)
```

```python
import functools
import math
from functools import reduce

import jax
import jax.numpy as jnp
import numpy as np
from jax import lax
from jax.experimental import pallas as pl
from jax.experimental.pallas import tpu as pltpu
from jax.sharding import PartitionSpec as P

ITERS = 2


cross_weight = 1.0 / 64.0


def extended_2(x, sides, width):
    for axis, dim in sides:
        devices, length = (lax.axis_size(axis), x.shape[dim])
        up = [(i, (i + 1) % devices) for i in range(devices - 1)]
        down = [(j, i) for i, j in up]
        last = lax.slice_in_dim(x, length - width, length, axis=dim)
        first = lax.slice_in_dim(x, 0, width, axis=dim)
        before = lax.ppermute(last, axis, up)
        after = lax.ppermute(first, axis, down)
        x = jnp.concatenate([before, x, after], axis=dim)
    return x


def coupling_tables(multi_index):
    upper_rows = multi_index[:, None, :]
    lower_rows = multi_index[None, :, :]
    offset = upper_rows - lower_rows
    distance = jnp.sum(jnp.abs(offset), axis=2)
    larger = jnp.maximum(upper_rows, lower_rows).astype(jnp.float32)
    adjacent = (jnp.abs(offset) == 1) & (distance == 1)[:, :, None]
    raising = jnp.where(adjacent, jnp.sqrt(larger), jnp.zeros_like(larger))
    identity = (distance == 0).astype(jnp.float32)
    coupling = jnp.concatenate([identity[None], jnp.transpose(raising, (2, 0, 1))], axis=0)
    mean_pick = (jnp.sum(multi_index, axis=1) == 0).astype(jnp.float32)
    return (coupling, mean_pick)


def neighbour_views(padded):
    return [
        padded[:, :, 2:, 1:-1, 1:-1],
        padded[:, :, :-2, 1:-1, 1:-1],
        padded[:, :, 1:-1, 2:, 1:-1],
        padded[:, :, 1:-1, :-2, 1:-1],
        padded[:, :, 1:-1, 1:-1, 2:],
        padded[:, :, 1:-1, 1:-1, :-2],
    ]


def face_list(fields, padded):
    weights = [1.0, 1.0, cross_weight, cross_weight, cross_weight, cross_weight]
    return [
        weight * 0.5 * (fields + beside) for weight, beside in zip(weights, neighbour_views(padded))
    ]


def line_prepare(main_band, sub_band, super_band):
    position = lax.broadcasted_iota(jnp.int32, main_band.shape, 1)
    sub_band = jnp.where(position == 0, jnp.zeros_like(sub_band), sub_band)
    super_band = jnp.where(
        position == main_band.shape[1] - 1, jnp.zeros_like(super_band), super_band
    )
    return tuple((jnp.moveaxis(band_arr, 1, 3) for band_arr in (sub_band, main_band, super_band)))


def line_solve(residual, prepared):
    sub_band, main_band, super_band = prepared
    stacked = jnp.transpose(residual, (0, 3, 4, 2, 1))
    solved = lax.linalg.tridiagonal_solve(sub_band, main_band, super_band, stacked)
    return jnp.transpose(solved, (0, 4, 3, 1, 2))


def pad_fields(fields):
    extended = extended_2(fields, (("space", 2),), 1)
    return jnp.pad(extended, ((0, 0), (0, 0), (0, 0), (1, 1), (1, 1)))


def pad_state(field_in):
    extended = extended_2(field_in, (("space", 2),), 1)
    return jnp.pad(extended, ((0, 0), (0, 0), (0, 0), (1, 1), (1, 1)))


def residual_fit(residual, smoothed):
    return lax.psum(jnp.sum(residual * smoothed, axis=(1, 2, 3, 4)), "space")


def spread(values):
    return values[:, None, None, None, None]


def plain_on_device(adjoint_source, kl_bank, multi_index, sample_ids):
    coupling, mean_pick = coupling_tables(multi_index)
    fields = jnp.take(kl_bank, sample_ids, axis=0)
    face_coefs = face_list(fields, pad_fields(fields))
    main_band = reduce(jnp.add, [coef[:, 0] for coef in face_coefs])
    sub_band = -face_coefs[1][:, 0]
    super_band = -face_coefs[0][:, 0]
    main_band, sub_band, super_band = (
        lax.all_to_all(main_band, "space", split_axis=3, concat_axis=1, tiled=True),
        lax.all_to_all(sub_band, "space", split_axis=3, concat_axis=1, tiled=True),
        lax.all_to_all(super_band, "space", split_axis=3, concat_axis=1, tiled=True),
    )
    prepared = line_prepare(main_band, sub_band, super_band)

    def precondition(residual):
        line_data = lax.all_to_all(residual, "space", split_axis=4, concat_axis=2, tiled=True)
        solved = line_solve(line_data, prepared)
        return lax.all_to_all(solved, "space", split_axis=2, concat_axis=4, tiled=True)

    def operate(field_in):
        views = neighbour_views(pad_state(field_in))
        weighted = reduce(
            jnp.add,
            [
                coef[:, :, None] * (field_in[:, None] - beside[:, None])
                for coef, beside in zip(face_coefs, views)
            ],
        )
        return jnp.einsum(
            "kij,skjxyz->sixyz",
            coupling,
            weighted,
            precision=lax.Precision.HIGHEST,
            preferred_element_type=jnp.float32,
        )

    solution = jnp.zeros_like(adjoint_source)
    residual = adjoint_source
    smoothed = precondition(residual)
    direction = smoothed
    fit_now = residual_fit(residual, smoothed)
    for iteration in range(ITERS):
        image_vec = operate(direction)
        curvature_sum = lax.psum(jnp.sum(direction * image_vec, axis=(1, 2, 3, 4)), "space")
        step_size = fit_now / curvature_sum
        solution = solution + spread(step_size) * direction
        residual = residual - spread(step_size) * image_vec
        if iteration + 1 < ITERS:
            smoothed = precondition(residual)
            fit_next = residual_fit(residual, smoothed)
            direction = smoothed + spread(fit_next / fit_now) * direction
            fit_now = fit_next
    sample_count = solution.shape[0] * lax.axis_size("sample")
    mean_term = (
        jnp.einsum(
            "p,spxyz->xyz",
            mean_pick,
            solution,
            precision=lax.Precision.HIGHEST,
            preferred_element_type=jnp.float32,
        )
        / sample_count
    )
    gradient = lax.psum_scatter(mean_term, "sample", scatter_dimension=1, tiled=True)
    return (solution, gradient)


DEGREE = 3
CELL_ROWS = 8
LANES = 128


def basis_rows(variables):
    rows = [[]]
    for _ in range(variables):
        rows = [row + [d] for row in rows for d in range(DEGREE + 1) if sum(row) + d <= DEGREE]
    return rows


def couplings(variables):
    rows = basis_rows(variables)
    place = {tuple(row): i for i, row in enumerate(rows)}
    result = []
    for row in rows:
        mine = []
        for k in range(variables):
            for change in (-1, 1):
                other = list(row)
                other[k] += change
                j = place.get(tuple(other))
                if j is not None:
                    mine.append((k + 1, j, math.sqrt(max(row[k], other[k]))))
        result.append(mine)
    return rows, result


def roll(x, shift, axis=1):
    shift %= x.shape[axis]
    return x if shift == 0 else pltpu.roll(x, shift, axis)


def kernel(
    slabs, samples, variables,
    sid_ref, idx_ref, src_ref, kl_ref,
    out_ref, grad_ref,
    f_send, f_recv, r_send, r_recv, b_send, b_recv,
    halo_send, halo_recv, sum_send, sum_recv, mean_send, mean_recv,
    coefs, z_vec, u_vec, q_vec, terms, x_vec,
    send_sem, recv_sem,
):
    rows, links = couplings(variables)
    modes = len(rows)
    mean_mode = rows.index([0] * variables)
    fields = variables + 1
    width = LANES // slabs
    me = lax.axis_index("space")
    mine = lax.axis_index("sample")

    lane = lax.broadcasted_iota(jnp.int32, (CELL_ROWS, LANES), 1)
    row = lax.broadcasted_iota(jnp.int32, (CELL_ROWS, LANES), 0)
    block = lane // width
    inner = lane % width
    is_block = [block == b for b in range(slabs)]
    low_edge, high_edge = inner == 0, inner == width - 1
    zero = jnp.zeros((CELL_ROWS, LANES), jnp.float32)

    def pack(values, dest):
        result = zero
        for j, value in enumerate(values):
            result = jnp.where(is_block[j], roll(value, (j - dest) * width), result)
        return result

    def unpack(values, j):
        result = zero
        for b, value in enumerate(values):
            result = jnp.where(is_block[b], roll(value, (b - j) * width), result)
        return result

    def exchange(send, recv, first):
        copies = []
        for away in range(1, slabs):
            dest = lax.rem(me + away, slabs)
            copies.append(
                pltpu.make_async_remote_copy(
                    src_ref=send.at[dest],
                    dst_ref=recv.at[me],
                    send_sem=send_sem.at[first + away - 1],
                    recv_sem=recv_sem.at[first + away - 1],
                    device_id={"space": dest},
                    device_id_type=pl.DeviceIdType.MESH,
                )
            )
        return copies

    halo_recv[...] = jnp.zeros_like(halo_recv)
    barrier = pltpu.get_barrier_semaphore()
    for away in range(1, slabs):
        pl.semaphore_signal(
            barrier, inc=1, device_id={"space": lax.rem(me + away, slabs)},
            device_id_type=pl.DeviceIdType.MESH,
        )
    for away in range(1, samples):
        pl.semaphore_signal(
            barrier, inc=1, device_id={"sample": lax.rem(mine + away, samples)},
            device_id_type=pl.DeviceIdType.MESH,
        )

    sid = sid_ref[0]
    chunks = [kl_ref[sid, k] for k in range(fields)]
    chunks = (
        chunks
        + [jnp.where(lane == LANES - 1, 0.0, roll(f, -1)) for f in chunks]
        + [jnp.where(lane == 0, 0.0, roll(f, 1)) for f in chunks]
    )
    for p in range(f_send.shape[1]):
        group = chunks[p * slabs:(p + 1) * slabs]
        for dest in range(slabs):
            f_send[dest, p] = pack(group, dest)
    f_recv[me] = f_send[me]

    pl.semaphore_wait(barrier, slabs - 1 + samples - 1)
    f_copies = exchange(f_send, f_recv, 0)
    for copy in f_copies:
        copy.start()

    groups = modes // slabs
    for p in range(groups):
        group = [src_ref[idx_ref[p * slabs + j]] for j in range(slabs)]
        for dest in range(slabs):
            r_send[dest, p] = pack(group, dest)
    r_recv[me] = r_send[me]
    r_copies = exchange(r_send, r_recv, slabs - 1)
    for copy in r_copies:
        copy.start()

    for copy in f_copies:
        copy.wait()

    def field(number):
        p, j = divmod(number, slabs)
        return unpack([f_recv[b, p] for b in range(slabs)], j)

    lowest = low_edge & (me == 0)
    highest = high_edge & (me == slabs - 1)
    mean_diag = mean_next = None
    for k in range(fields):
        f = field(k)
        xp = 0.5 * (f + jnp.where(is_block[slabs - 1], 0.0, roll(f, -width)))
        xm = 0.5 * (f + jnp.where(is_block[0], 0.0, roll(f, width)))
        half = 0.5 * cross_weight
        yp = half * (f + jnp.where(row == CELL_ROWS - 1, 0.0, roll(f, -1, 0)))
        ym = half * (f + jnp.where(row == 0, 0.0, roll(f, 1, 0)))
        zp = half * (f + field(fields + k))
        zm = half * (f + field(2 * fields + k))
        diag = xp + xm + yp + ym + zp + zm
        if k == 0:
            mean_diag, mean_next = diag, xp
        coefs[k, 0] = diag
        coefs[k, 1] = jnp.where(is_block[slabs - 1], 0.0, xp)
        coefs[k, 2] = jnp.where(is_block[0], 0.0, xm)
        coefs[k, 3] = jnp.where(row == CELL_ROWS - 1, 0.0, yp)
        coefs[k, 4] = jnp.where(row == 0, 0.0, ym)
        coefs[k, 5] = jnp.where(highest, 0.0, zp)
        coefs[k, 6] = jnp.where(lowest, 0.0, zm)

    d = [unpack([mean_diag] * slabs, x) for x in range(slabs)]
    a = [unpack([mean_next] * slabs, x) for x in range(slabs - 1)]
    one = jnp.ones_like(zero)
    lead = [one, d[0]]
    for x in range(1, slabs):
        lead.append(d[x] * lead[x] - a[x - 1] * a[x - 1] * lead[x - 1])
    trail = [one, d[slabs - 1]]
    for x in range(slabs - 2, -1, -1):
        trail.append(d[x] * trail[-1] - a[x] * a[x] * trail[-2])
    trail = trail[::-1]
    scale = one / lead[slabs]
    inverse = {}
    for i in range(slabs):
        between = scale
        for j in range(i, slabs):
            if j > i:
                between = between * a[j - 1]
            inverse[i, j] = inverse[j, i] = between * lead[i] * trail[j + 1]
    line = []
    for shift in range(slabs):
        weight = zero
        for x in range(slabs):
            weight = jnp.where(is_block[x], inverse[x, (x - shift) % slabs], weight)
        line.append(weight)

    def line_inverse(value):
        result = line[0] * value
        for shift in range(1, slabs):
            result = result + line[shift] * roll(value, shift * width)
        return result

    def send_halo(vec, number):
        packs = halo_send.shape[2]
        for p in range(packs):
            up = down = zero
            for m in range(p * width, min(modes, (p + 1) * width)):
                spot = m % width
                value = vec[m]
                up = jnp.where(inner == spot, roll(value, spot - (width - 1)), up)
                down = jnp.where(inner == spot, roll(value, spot), down)
            halo_send[number, 0, p] = up
            halo_send[number, 1, p] = down
        first = 2 * (slabs - 1) + 2 * number
        copies = []
        for way, step in ((0, 1), (1, slabs - 1)):
            copies.append(
                pltpu.make_async_remote_copy(
                    src_ref=halo_send.at[number, way],
                    dst_ref=halo_recv.at[number, way],
                    send_sem=send_sem.at[first + way],
                    recv_sem=recv_sem.at[first + way],
                    device_id={"space": lax.rem(me + step, slabs)},
                    device_id_type=pl.DeviceIdType.MESH,
                )
            )
        up, down = copies

        @pl.when(me < slabs - 1)
        def _():
            up.start()

        @pl.when(me > 0)
        def _():
            down.start()

        return up, down

    def wait_halo(copies):
        up, down = copies

        @pl.when(me < slabs - 1)
        def _():
            up.wait_send()
            down.wait_recv()

        @pl.when(me > 0)
        def _():
            down.wait_send()
            up.wait_recv()

    needed = [set() for _ in range(modes)]
    for i in range(modes):
        for k, j, _ in links[i]:
            needed[j].add(k)

    def rest_terms(vec, number):
        for m in range(modes):
            value = vec[m]
            p, spot = divmod(m, width)
            above = roll(halo_recv[number, 1, p], width - 1 - spot)
            below = roll(halo_recv[number, 0, p], -spot)
            beside = [
                roll(value, -width), roll(value, width), roll(value, -1, 0), roll(value, 1, 0),
                jnp.where(high_edge, above, roll(value, -1)),
                jnp.where(low_edge, below, roll(value, 1)),
            ]
            mean = zero
            for face in range(2, 6):
                mean = mean - coefs[0, 1 + face] * beside[face]
            terms[0, m] = mean
            for k in sorted(needed[m]):
                total = coefs[k, 0] * value
                for face in range(6):
                    total = total - coefs[k, 1 + face] * beside[face]
                terms[k, m] = total

    def coupled(i):
        total = terms[0, i]
        by_weight = {}
        for k, j, weight in links[i]:
            by_weight.setdefault(weight, []).append((k, j))
        for weight, pairs in by_weight.items():
            part = terms[pairs[0][0], pairs[0][1]]
            for k, j in pairs[1:]:
                part = part + terms[k, j]
            total = total + (part if weight == 1.0 else np.float32(weight) * part)
        return total

    for copy in r_copies:
        copy.wait()
    fit = zero
    for p in range(groups):
        values = [r_recv[b, p] for b in range(slabs)]
        for j in range(slabs):
            residual = unpack(values, j)
            smoothed = line_inverse(residual)
            z_vec[p * slabs + j] = smoothed
            fit = fit + residual * smoothed
    copies = send_halo(z_vec, 0)
    wait_halo(copies)
    rest_terms(z_vec, 0)
    cross = square = zero
    for i in range(modes):
        rest = coupled(i)
        smoothed = line_inverse(rest)
        u_vec[i] = smoothed
        cross = cross + z_vec[i] * rest
        square = square + rest * smoothed
    copies = send_halo(u_vec, 1)
    wait_halo(copies)
    rest_terms(u_vec, 1)
    last = zero
    for i in range(modes):
        last = last + u_vec[i] * coupled(i)

    sums = zero
    for number, value in enumerate((fit, cross, square, last)):
        sums = jnp.where(row == number, jnp.sum(value, axis=0, keepdims=True), sums)
    sum_send[...] = sums
    first = 2 * (slabs - 1) + 4
    sum_copies = []
    for away in range(1, slabs):
        dest = lax.rem(me + away, slabs)
        sum_copies.append(
            pltpu.make_async_remote_copy(
                src_ref=sum_send,
                dst_ref=sum_recv.at[me],
                send_sem=send_sem.at[first + away - 1],
                recv_sem=recv_sem.at[first + away - 1],
                device_id={"space": dest},
                device_id_type=pl.DeviceIdType.MESH,
            )
        )
    for copy in sum_copies:
        copy.start()
    sum_recv[me] = sums
    for copy in sum_copies:
        copy.wait()
    sums = jnp.sum(reduce(jnp.add, [sum_recv[b] for b in range(slabs)]), axis=1, keepdims=True)
    f, e, g, h = (jnp.broadcast_to(sums[n:n + 1], zero.shape) for n in range(4))
    curve = f + e
    step = f / curve
    ratio = (f * g - e * e) / (curve * curve)
    z_part = e / curve + ratio
    curve_next = (
        z_part * z_part * curve - 2.0 * z_part * step * (e + g) + step * step * (g + h)
    )
    step_next = ratio * f / curve_next
    z_part = step + step_next * z_part
    u_part = -step_next * step

    for p in range(groups):
        group = [
            z_part * z_vec[p * slabs + j] + u_part * u_vec[p * slabs + j] for j in range(slabs)
        ]
        for dest in range(slabs):
            b_send[dest, p] = pack(group, dest)
    b_recv[me] = b_send[me]
    first += slabs - 1
    b_copies = exchange(b_send, b_recv, first)
    for copy in b_copies:
        copy.start()
    for copy in b_copies:
        copy.wait()

    first += slabs - 1
    p, j = divmod(mean_mode, slabs)
    mean = unpack([b_recv[b, p] for b in range(slabs)], j)
    mean_send[...] = mean
    mean_copies = []
    for away in range(1, samples):
        mean_copies.append(
            pltpu.make_async_remote_copy(
                src_ref=mean_send,
                dst_ref=mean_recv.at[mine],
                send_sem=send_sem.at[first + away - 1],
                recv_sem=recv_sem.at[first + away - 1],
                device_id={"sample": lax.rem(mine + away, samples)},
                device_id_type=pl.DeviceIdType.MESH,
            )
        )
    for copy in mean_copies:
        copy.start()
    mean_recv[mine] = mean
    for p in range(groups):
        values = [b_recv[b, p] for b in range(slabs)]
        for j in range(slabs):
            x_vec[p * slabs + j] = unpack(values, j)
    for i in range(modes):
        out_ref[i] = x_vec[idx_ref[modes + i]]
    for copy in mean_copies:
        copy.wait()
    total = reduce(jnp.add, [mean_recv[b] for b in range(samples)]) * (1.0 / samples)
    share = CELL_ROWS // samples
    result = total[0:share]
    for b in range(1, samples):
        result = jnp.where(mine == b, total[b * share:(b + 1) * share], result)
    grad_ref[...] = result


def fused_on_device(adjoint_source, kl_bank, multi_index, sample_ids):
    slabs, samples = lax.axis_size("space"), lax.axis_size("sample")
    modes, variables = multi_index.shape
    fields = variables + 1
    base = DEGREE + 1
    places = np.array([base ** k for k in range(variables)], np.int32)
    codes = jnp.asarray(np.array(basis_rows(variables), np.int32) @ places)
    same = codes[:, None] == jnp.sum(multi_index * places, axis=1)[None, :]
    numbers = jnp.arange(modes, dtype=jnp.int32)
    index = jnp.concatenate(
        [
            jnp.sum(jnp.where(same, numbers[None, :], 0), axis=1),
            jnp.sum(jnp.where(same, numbers[:, None], 0), axis=0),
        ]
    )
    tile = (CELL_ROWS, LANES)
    groups = modes // slabs
    f_groups = -(-3 * fields // slabs)
    halos = -(-modes // (LANES // slabs))
    vmem = lambda *shape: pltpu.VMEM(shape + tile, jnp.float32)
    sems = 4 * (slabs - 1) + 4 + samples - 1
    in_vmem = pl.BlockSpec(memory_space=pltpu.VMEM)
    in_smem = pl.BlockSpec(memory_space=pltpu.SMEM)
    state, gradient = pl.pallas_call(
        functools.partial(kernel, slabs, samples, variables),
        out_shape=(
            jax.ShapeDtypeStruct((modes,) + tile, jnp.float32),
            jax.ShapeDtypeStruct((CELL_ROWS // samples, LANES), jnp.float32),
        ),
        in_specs=[in_smem, in_smem, in_vmem, in_vmem],
        out_specs=(in_vmem, in_vmem),
        scratch_shapes=[
            vmem(slabs, f_groups), vmem(slabs, f_groups),
            vmem(slabs, groups), vmem(slabs, groups),
            vmem(slabs, groups), vmem(slabs, groups),
            vmem(2, 2, halos), vmem(2, 2, halos),
            vmem(), vmem(slabs), vmem(), vmem(samples),
            vmem(fields, 7), vmem(modes), vmem(modes), vmem(modes), vmem(fields, modes),
            vmem(modes),
            pltpu.SemaphoreType.DMA((sems,)), pltpu.SemaphoreType.DMA((sems,)),
        ],
        compiler_params=pltpu.CompilerParams(
            collective_id=0, has_side_effects=True, vmem_limit_bytes=24 << 20
        ),
    )(
        sample_ids,
        index,
        adjoint_source.reshape((modes,) + tile),
        kl_bank.reshape(kl_bank.shape[:2] + tile),
    )
    return state.reshape(adjoint_source.shape), gradient[None]


def on_device(adjoint_source, kl_bank, multi_index, sample_ids):
    slabs, samples = lax.axis_size("space"), lax.axis_size("sample")
    modes, variables = multi_index.shape
    fits = (
        adjoint_source.shape == (1, modes, 1, CELL_ROWS, LANES)
        and slabs == 4
        and CELL_ROWS % samples == 0
        and samples > 1
        and modes % slabs == 0
        and modes == len(basis_rows(variables))
    )
    work = fused_on_device if fits else plain_on_device
    return work(adjoint_source, kl_bank, multi_index, sample_ids)


def solution(mesh):
    return jax.shard_map(
        on_device,
        mesh=mesh,
        in_specs=(
            P(("groups", "sample"), None, "space", None, None),
            P(None, None, "space", None, None),
            P(),
            P(("groups", "sample")),
        ),
        out_specs=(
            P(("groups", "sample"), None, "space", None, None),
            P(("groups", "space"), "sample", None),
        ),
        check_vma=False,
    )
```

```python
import functools
import math
from functools import reduce

import jax
import jax.numpy as jnp
import numpy as np
from jax import lax
from jax.experimental import pallas as pl
from jax.experimental.pallas import tpu as pltpu
from jax.sharding import PartitionSpec as P

ITERS = 2


cross_weight = 1.0 / 64.0


def extended_2(x, sides, width):
    for axis, dim in sides:
        devices, length = (lax.axis_size(axis), x.shape[dim])
        up = [(i, (i + 1) % devices) for i in range(devices - 1)]
        down = [(j, i) for i, j in up]
        last = lax.slice_in_dim(x, length - width, length, axis=dim)
        first = lax.slice_in_dim(x, 0, width, axis=dim)
        before = lax.ppermute(last, axis, up)
        after = lax.ppermute(first, axis, down)
        x = jnp.concatenate([before, x, after], axis=dim)
    return x


def coupling_tables(multi_index):
    upper_rows = multi_index[:, None, :]
    lower_rows = multi_index[None, :, :]
    offset = upper_rows - lower_rows
    distance = jnp.sum(jnp.abs(offset), axis=2)
    larger = jnp.maximum(upper_rows, lower_rows).astype(jnp.float32)
    adjacent = (jnp.abs(offset) == 1) & (distance == 1)[:, :, None]
    raising = jnp.where(adjacent, jnp.sqrt(larger), jnp.zeros_like(larger))
    identity = (distance == 0).astype(jnp.float32)
    coupling = jnp.concatenate([identity[None], jnp.transpose(raising, (2, 0, 1))], axis=0)
    mean_pick = (jnp.sum(multi_index, axis=1) == 0).astype(jnp.float32)
    return (coupling, mean_pick)


def neighbour_views(padded):
    return [
        padded[:, :, 2:, 1:-1, 1:-1],
        padded[:, :, :-2, 1:-1, 1:-1],
        padded[:, :, 1:-1, 2:, 1:-1],
        padded[:, :, 1:-1, :-2, 1:-1],
        padded[:, :, 1:-1, 1:-1, 2:],
        padded[:, :, 1:-1, 1:-1, :-2],
    ]


def face_list(fields, padded):
    weights = [1.0, 1.0, cross_weight, cross_weight, cross_weight, cross_weight]
    return [
        weight * 0.5 * (fields + beside) for weight, beside in zip(weights, neighbour_views(padded))
    ]


def line_prepare(main_band, sub_band, super_band):
    position = lax.broadcasted_iota(jnp.int32, main_band.shape, 1)
    sub_band = jnp.where(position == 0, jnp.zeros_like(sub_band), sub_band)
    super_band = jnp.where(
        position == main_band.shape[1] - 1, jnp.zeros_like(super_band), super_band
    )
    return tuple((jnp.moveaxis(band_arr, 1, 3) for band_arr in (sub_band, main_band, super_band)))


def line_solve(residual, prepared):
    sub_band, main_band, super_band = prepared
    stacked = jnp.transpose(residual, (0, 3, 4, 2, 1))
    solved = lax.linalg.tridiagonal_solve(sub_band, main_band, super_band, stacked)
    return jnp.transpose(solved, (0, 4, 3, 1, 2))


def pad_fields(fields):
    extended = extended_2(fields, (("space", 2),), 1)
    return jnp.pad(extended, ((0, 0), (0, 0), (0, 0), (1, 1), (1, 1)))


def pad_state(field_in):
    extended = extended_2(field_in, (("space", 2),), 1)
    return jnp.pad(extended, ((0, 0), (0, 0), (0, 0), (1, 1), (1, 1)))


def residual_fit(residual, smoothed):
    return lax.psum(jnp.sum(residual * smoothed, axis=(1, 2, 3, 4)), "space")


def spread(values):
    return values[:, None, None, None, None]


def plain_on_device(adjoint_source, kl_bank, multi_index, sample_ids):
    coupling, mean_pick = coupling_tables(multi_index)
    fields = jnp.take(kl_bank, sample_ids, axis=0)
    face_coefs = face_list(fields, pad_fields(fields))
    main_band = reduce(jnp.add, [coef[:, 0] for coef in face_coefs])
    sub_band = -face_coefs[1][:, 0]
    super_band = -face_coefs[0][:, 0]
    main_band, sub_band, super_band = (
        lax.all_to_all(main_band, "space", split_axis=3, concat_axis=1, tiled=True),
        lax.all_to_all(sub_band, "space", split_axis=3, concat_axis=1, tiled=True),
        lax.all_to_all(super_band, "space", split_axis=3, concat_axis=1, tiled=True),
    )
    prepared = line_prepare(main_band, sub_band, super_band)

    def precondition(residual):
        line_data = lax.all_to_all(residual, "space", split_axis=4, concat_axis=2, tiled=True)
        solved = line_solve(line_data, prepared)
        return lax.all_to_all(solved, "space", split_axis=2, concat_axis=4, tiled=True)

    def operate(field_in):
        views = neighbour_views(pad_state(field_in))
        weighted = reduce(
            jnp.add,
            [
                coef[:, :, None] * (field_in[:, None] - beside[:, None])
                for coef, beside in zip(face_coefs, views)
            ],
        )
        return jnp.einsum(
            "kij,skjxyz->sixyz",
            coupling,
            weighted,
            precision=lax.Precision.HIGHEST,
            preferred_element_type=jnp.float32,
        )

    solution = jnp.zeros_like(adjoint_source)
    residual = adjoint_source
    smoothed = precondition(residual)
    direction = smoothed
    fit_now = residual_fit(residual, smoothed)
    for iteration in range(ITERS):
        image_vec = operate(direction)
        curvature_sum = lax.psum(jnp.sum(direction * image_vec, axis=(1, 2, 3, 4)), "space")
        step_size = fit_now / curvature_sum
        solution = solution + spread(step_size) * direction
        residual = residual - spread(step_size) * image_vec
        if iteration + 1 < ITERS:
            smoothed = precondition(residual)
            fit_next = residual_fit(residual, smoothed)
            direction = smoothed + spread(fit_next / fit_now) * direction
            fit_now = fit_next
    sample_count = solution.shape[0] * lax.axis_size("sample")
    mean_term = (
        jnp.einsum(
            "p,spxyz->xyz",
            mean_pick,
            solution,
            precision=lax.Precision.HIGHEST,
            preferred_element_type=jnp.float32,
        )
        / sample_count
    )
    gradient = lax.psum_scatter(mean_term, "sample", scatter_dimension=1, tiled=True)
    return (solution, gradient)


DEGREE = 3
CELL_ROWS = 8
LANES = 128


def basis_rows(variables):
    rows = [[]]
    for _ in range(variables):
        rows = [row + [d] for row in rows for d in range(DEGREE + 1) if sum(row) + d <= DEGREE]
    return rows


def couplings(variables):
    rows = basis_rows(variables)
    place = {tuple(row): i for i, row in enumerate(rows)}
    result = []
    for row in rows:
        mine = []
        for k in range(variables):
            for change in (-1, 1):
                other = list(row)
                other[k] += change
                j = place.get(tuple(other))
                if j is not None:
                    mine.append((k + 1, j, math.sqrt(max(row[k], other[k]))))
        result.append(mine)
    return rows, result


def roll(x, shift, axis=1):
    shift %= x.shape[axis]
    return x if shift == 0 else pltpu.roll(x, shift, axis)


def kernel(
    slabs, samples, variables,
    sid_ref, idx_ref, src_hbm, kl_hbm,
    out_ref, grad_ref,
    src_ref, kl_ref, f_send, f_recv, r_send, r_recv, zx_send, zx_recv, ux_send, ux_recv,
    halo_send, halo_recv, sum_send, sum_recv, mean_send, mean_recv,
    coefs, z_vec, u_vec, terms, zx_vec, ux_vec,
    send_sem, recv_sem, load_sem,
):
    rows, links = couplings(variables)
    modes = len(rows)
    mean_mode = rows.index([0] * variables)
    fields = variables + 1
    width = LANES // slabs
    me = lax.axis_index("space")
    mine = lax.axis_index("sample")

    lane = lax.broadcasted_iota(jnp.int32, (CELL_ROWS, LANES), 1)
    row = lax.broadcasted_iota(jnp.int32, (CELL_ROWS, LANES), 0)
    block = lane // width
    inner = lane % width
    is_block = [block == b for b in range(slabs)]
    low_edge, high_edge = inner == 0, inner == width - 1
    zero = jnp.zeros((CELL_ROWS, LANES), jnp.float32)

    def pack(values, dest):
        result = zero
        for j, value in enumerate(values):
            result = jnp.where(is_block[j], roll(value, (j - dest) * width), result)
        return result

    def unpack(values, j):
        result = zero
        for b, value in enumerate(values):
            result = jnp.where(is_block[b], roll(value, (b - j) * width), result)
        return result

    def exchange(send, recv, first):
        copies = []
        for away in range(1, slabs):
            dest = lax.rem(me + away, slabs)
            copies.append(
                pltpu.make_async_remote_copy(
                    src_ref=send.at[dest],
                    dst_ref=recv.at[me],
                    send_sem=send_sem.at[first + away - 1],
                    recv_sem=recv_sem.at[first + away - 1],
                    device_id={"space": dest},
                    device_id_type=pl.DeviceIdType.MESH,
                )
            )
        return copies

    loads = [
        pltpu.make_async_copy(kl_hbm, kl_ref, load_sem.at[0]),
        pltpu.make_async_copy(src_hbm, src_ref, load_sem.at[1]),
    ]
    for load in loads:
        load.start()
    halo_recv[...] = jnp.zeros_like(halo_recv)
    barrier = pltpu.get_barrier_semaphore()
    others = [(x, y) for x in range(samples) for y in range(slabs) if x or y]
    peers = [(lax.rem(mine + x, samples), lax.rem(me + y, slabs)) for x, y in others]
    for sample, slab in peers:
        pl.semaphore_signal(
            barrier, inc=1, device_id={"sample": sample, "space": slab},
            device_id_type=pl.DeviceIdType.MESH,
        )

    loads[0].wait()
    sid = sid_ref[0]
    chunks = [kl_ref[sid, k] for k in range(fields)]
    chunks = (
        chunks
        + [jnp.where(lane == LANES - 1, 0.0, roll(f, -1)) for f in chunks]
        + [jnp.where(lane == 0, 0.0, roll(f, 1)) for f in chunks]
    )
    for p in range(f_send.shape[1]):
        group = chunks[p * slabs:(p + 1) * slabs]
        for dest in range(slabs):
            f_send[dest, p] = pack(group, dest)
    f_recv[me] = f_send[me]

    pl.semaphore_wait(barrier, len(peers))
    f_copies = exchange(f_send, f_recv, 0)
    for copy in f_copies:
        copy.start()

    groups = modes // slabs
    def pack_all(load, send):
        for q in range(0, groups, 4):
            batch = range(q, min(groups, q + 4))
            values = [[load(p * slabs + j) for j in range(slabs)] for p in batch]
            packed = [[pack(group, dest) for dest in range(slabs)] for group in values]
            for p, row_packed in zip(batch, packed):
                for dest in range(slabs):
                    send[dest, p] = row_packed[dest]
        send_own = send[me]
        return send_own

    def unpack_all(recv, vec):
        for q in range(0, groups, 4):
            batch = range(q, min(groups, q + 4))
            values = [[recv[b, p] for b in range(slabs)] for p in batch]
            values = [unpack(group, j) for group in values for j in range(slabs)]
            for n, value in enumerate(values):
                vec[q * slabs + n] = value

    loads[1].wait()
    r_recv[me] = pack_all(lambda m: src_ref[idx_ref[m]], r_send)
    r_copies = exchange(r_send, r_recv, slabs - 1)
    for copy in r_copies:
        copy.start()

    for copy in f_copies:
        copy.wait()

    def field(number):
        p, j = divmod(number, slabs)
        return unpack([f_recv[b, p] for b in range(slabs)], j)

    lowest = low_edge & (me == 0)
    highest = high_edge & (me == slabs - 1)
    mean_diag = mean_next = None
    for k in range(fields):
        f = field(k)
        xp = 0.5 * (f + jnp.where(is_block[slabs - 1], 0.0, roll(f, -width)))
        xm = 0.5 * (f + jnp.where(is_block[0], 0.0, roll(f, width)))
        half = 0.5 * cross_weight
        yp = half * (f + jnp.where(row == CELL_ROWS - 1, 0.0, roll(f, -1, 0)))
        ym = half * (f + jnp.where(row == 0, 0.0, roll(f, 1, 0)))
        zp = half * (f + field(fields + k))
        zm = half * (f + field(2 * fields + k))
        diag = xp + xm + yp + ym + zp + zm
        if k == 0:
            mean_diag, mean_next = diag, xp
        coefs[k, 0] = diag
        coefs[k, 1] = jnp.where(is_block[slabs - 1], 0.0, xp)
        coefs[k, 2] = jnp.where(is_block[0], 0.0, xm)
        coefs[k, 3] = jnp.where(row == CELL_ROWS - 1, 0.0, yp)
        coefs[k, 4] = jnp.where(row == 0, 0.0, ym)
        coefs[k, 5] = jnp.where(highest, 0.0, zp)
        coefs[k, 6] = jnp.where(lowest, 0.0, zm)

    d = [unpack([mean_diag] * slabs, x) for x in range(slabs)]
    a = [unpack([mean_next] * slabs, x) for x in range(slabs - 1)]
    one = jnp.ones_like(zero)
    lead = [one, d[0]]
    for x in range(1, slabs):
        lead.append(d[x] * lead[x] - a[x - 1] * a[x - 1] * lead[x - 1])
    trail = [one, d[slabs - 1]]
    for x in range(slabs - 2, -1, -1):
        trail.append(d[x] * trail[-1] - a[x] * a[x] * trail[-2])
    trail = trail[::-1]
    scale = one / lead[slabs]
    inverse = {}
    for i in range(slabs):
        between = scale
        for j in range(i, slabs):
            if j > i:
                between = between * a[j - 1]
            inverse[i, j] = inverse[j, i] = between * lead[i] * trail[j + 1]
    line = []
    for shift in range(slabs):
        weight = zero
        for x in range(slabs):
            weight = jnp.where(is_block[x], inverse[x, (x - shift) % slabs], weight)
        line.append(weight)

    def line_inverse(value):
        result = line[0] * value
        for shift in range(1, slabs):
            result = result + line[shift] * roll(value, shift * width)
        return result

    def send_halo(vec, number):
        packs = halo_send.shape[2]
        for p in range(packs):
            up = down = zero
            for m in range(p * width, min(modes, (p + 1) * width)):
                spot = m % width
                value = vec[m]
                up = jnp.where(inner == spot, roll(value, spot - (width - 1)), up)
                down = jnp.where(inner == spot, roll(value, spot), down)
            halo_send[number, 0, p] = up
            halo_send[number, 1, p] = down
        first = 2 * (slabs - 1) + 2 * number
        copies = []
        for way, step in ((0, 1), (1, slabs - 1)):
            copies.append(
                pltpu.make_async_remote_copy(
                    src_ref=halo_send.at[number, way],
                    dst_ref=halo_recv.at[number, way],
                    send_sem=send_sem.at[first + way],
                    recv_sem=recv_sem.at[first + way],
                    device_id={"space": lax.rem(me + step, slabs)},
                    device_id_type=pl.DeviceIdType.MESH,
                )
            )
        up, down = copies

        @pl.when(me < slabs - 1)
        def _():
            up.start()

        @pl.when(me > 0)
        def _():
            down.start()

        return up, down

    def wait_halo(copies):
        up, down = copies

        @pl.when(me < slabs - 1)
        def _():
            up.wait_send()
            down.wait_recv()

        @pl.when(me > 0)
        def _():
            down.wait_send()
            up.wait_recv()

    needed = [set() for _ in range(modes)]
    for i in range(modes):
        for k, j, _ in links[i]:
            needed[j].add(k)

    def rest_terms(vec, number):
        for q in range(0, modes, 4):
            batch = range(q, min(modes, q + 4))
            values = [vec[m] for m in batch]
            sides = []
            for m, value in zip(batch, values):
                p, spot = divmod(m, width)
                above = roll(halo_recv[number, 1, p], width - 1 - spot)
                below = roll(halo_recv[number, 0, p], -spot)
                sides.append([
                    roll(value, -width), roll(value, width), roll(value, -1, 0), roll(value, 1, 0),
                    jnp.where(high_edge, above, roll(value, -1)),
                    jnp.where(low_edge, below, roll(value, 1)),
                ])
            results = {}
            for k in range(fields):
                factor = [coefs[k, n] for n in range(7)]
                for m, value, beside in zip(batch, values, sides):
                    if k == 0:
                        results[k, m] = -(
                            (factor[3] * beside[2] + factor[4] * beside[3])
                            + (factor[5] * beside[4] + factor[6] * beside[5])
                        )
                    elif k in needed[m]:
                        parts = [factor[1 + face] * beside[face] for face in range(6)]
                        results[k, m] = factor[0] * value - (
                            (parts[0] + parts[1]) + (parts[2] + parts[3]) + (parts[4] + parts[5])
                        )
            for (k, m), result in results.items():
                terms[k, m] = result

    def coupled(i):
        total = terms[0, i]
        by_weight = {}
        for k, j, weight in links[i]:
            by_weight.setdefault(weight, []).append((k, j))
        for weight, pairs in by_weight.items():
            part = terms[pairs[0][0], pairs[0][1]]
            for k, j in pairs[1:]:
                part = part + terms[k, j]
            total = total + (part if weight == 1.0 else np.float32(weight) * part)
        return total

    for copy in r_copies:
        copy.wait()
    fit = zero
    for q in range(0, groups, 4):
        batch = range(q, min(groups, q + 4))
        values = [[r_recv[b, p] for b in range(slabs)] for p in batch]
        residuals = [unpack(group, j) for group in values for j in range(slabs)]
        results = [line_inverse(residual) for residual in residuals]
        for n, (residual, smoothed) in enumerate(zip(residuals, results)):
            z_vec[q * slabs + n] = smoothed
            fit = fit + residual * smoothed
    copies = send_halo(z_vec, 0)
    first = 2 * (slabs - 1) + 4
    zx_recv[me] = pack_all(lambda m: z_vec[m], zx_send)
    zx_copies = exchange(zx_send, zx_recv, first)
    for copy in zx_copies:
        copy.start()
    wait_halo(copies)
    rest_terms(z_vec, 0)
    cross = square = zero
    for q in range(0, modes, 8):
        batch = range(q, min(modes, q + 8))
        rests = [coupled(i) for i in batch]
        results = [line_inverse(rest) for rest in rests]
        for i, rest, smoothed in zip(batch, rests, results):
            u_vec[i] = smoothed
            cross = cross + z_vec[i] * rest
            square = square + rest * smoothed
    copies = send_halo(u_vec, 1)
    first += slabs - 1
    ux_recv[me] = pack_all(lambda m: u_vec[m], ux_send)
    ux_copies = exchange(ux_send, ux_recv, first)
    for copy in ux_copies:
        copy.start()
    wait_halo(copies)
    rest_terms(u_vec, 1)
    last = [zero] * 4
    for i in range(modes):
        last[i % 4] = last[i % 4] + u_vec[i] * coupled(i)
    last = (last[0] + last[1]) + (last[2] + last[3])

    sums = zero
    for number, value in enumerate((fit, cross, square, last)):
        sums = jnp.where(row == number, jnp.sum(value, axis=0, keepdims=True), sums)
    sum_send[...] = sums
    first += slabs - 1
    sum_copies = []
    for n, (sample, slab) in enumerate(peers):
        sum_copies.append(
            pltpu.make_async_remote_copy(
                src_ref=sum_send,
                dst_ref=sum_recv.at[mine, me],
                send_sem=send_sem.at[first + n],
                recv_sem=recv_sem.at[first + n],
                device_id={"sample": sample, "space": slab},
                device_id_type=pl.DeviceIdType.MESH,
            )
        )
    for copy in sum_copies:
        copy.start()
    sum_recv[mine, me] = sums

    for copy in zx_copies:
        copy.wait()
    unpack_all(zx_recv, zx_vec)
    for copy in ux_copies:
        copy.wait()
    p, j = divmod(mean_mode, slabs)
    mean_send[0] = zx_vec[mean_mode]
    mean_send[1] = unpack([ux_recv[b, p] for b in range(slabs)], j)
    first += len(peers)
    mean_copies = []
    for away in range(1, samples):
        mean_copies.append(
            pltpu.make_async_remote_copy(
                src_ref=mean_send,
                dst_ref=mean_recv.at[mine],
                send_sem=send_sem.at[first + away - 1],
                recv_sem=recv_sem.at[first + away - 1],
                device_id={"sample": lax.rem(mine + away, samples)},
                device_id_type=pl.DeviceIdType.MESH,
            )
        )
    for copy in mean_copies:
        copy.start()
    mean_recv[mine] = mean_send[...]
    unpack_all(ux_recv, ux_vec)
    for copy in sum_copies:
        copy.wait()

    def parts(sample):
        total = reduce(jnp.add, [sum_recv[sample, b] for b in range(slabs)])
        total = jnp.sum(total, axis=1, keepdims=True)
        f, e, g, h = (jnp.broadcast_to(total[n:n + 1], zero.shape) for n in range(4))
        curve = f + e
        step = f / curve
        ratio = (f * g - e * e) / (curve * curve)
        z_part = e / curve + ratio
        curve_next = (
            z_part * z_part * curve - 2.0 * z_part * step * (e + g) + step * step * (g + h)
        )
        step_next = ratio * f / curve_next
        return step + step_next * z_part, -step_next * step

    z_part, u_part = parts(mine)
    for q in range(0, modes, 8):
        batch = range(q, min(modes, q + 8))
        places = [idx_ref[modes + i] for i in batch]
        results = [z_part * zx_vec[place] + u_part * ux_vec[place] for place in places]
        for i, result in zip(batch, results):
            out_ref[i] = result
    for copy in mean_copies:
        copy.wait()
    total = zero
    for sample in range(samples):
        z_part, u_part = parts(sample)
        total = total + (z_part * mean_recv[sample, 0] + u_part * mean_recv[sample, 1])
    total = total * (1.0 / samples)
    share = CELL_ROWS // samples
    result = total[0:share]
    for b in range(1, samples):
        result = jnp.where(mine == b, total[b * share:(b + 1) * share], result)
    grad_ref[...] = result


def fused_on_device(adjoint_source, kl_bank, multi_index, sample_ids):
    slabs, samples = lax.axis_size("space"), lax.axis_size("sample")
    modes, variables = multi_index.shape
    fields = variables + 1
    code = reduce(lambda c, k: c * (DEGREE + 1) + multi_index[:, k], range(variables), 0)
    numbers = jnp.arange(modes, dtype=jnp.int32)
    rank = jnp.sum((code[None, :] < code[:, None]).astype(jnp.int32), axis=1)
    source = jnp.sum(jnp.where(rank[None, :] == numbers[:, None], numbers[None, :], 0), axis=1)
    index = jnp.concatenate([source, rank])
    tile = (CELL_ROWS, LANES)
    groups = modes // slabs
    f_groups = -(-3 * fields // slabs)
    halos = -(-modes // (LANES // slabs))
    vmem = lambda *shape: pltpu.VMEM(shape + tile, jnp.float32)
    sems = 4 * (slabs - 1) + 4 + slabs * samples - 1 + samples - 1
    in_vmem = pl.BlockSpec(memory_space=pltpu.VMEM)
    in_hbm = pl.BlockSpec(memory_space=pltpu.HBM)
    in_smem = pl.BlockSpec(memory_space=pltpu.SMEM)
    state, gradient = pl.pallas_call(
        functools.partial(kernel, slabs, samples, variables),
        out_shape=(
            jax.ShapeDtypeStruct((modes,) + tile, jnp.float32),
            jax.ShapeDtypeStruct((CELL_ROWS // samples, LANES), jnp.float32),
        ),
        in_specs=[in_smem, in_smem, in_hbm, in_hbm],
        out_specs=(in_vmem, in_vmem),
        scratch_shapes=[
            vmem(modes), vmem(*kl_bank.shape[:2]),
            vmem(slabs, f_groups), vmem(slabs, f_groups),
            vmem(slabs, groups), vmem(slabs, groups),
            vmem(slabs, groups), vmem(slabs, groups),
            vmem(slabs, groups), vmem(slabs, groups),
            vmem(2, 2, halos), vmem(2, 2, halos),
            vmem(), vmem(samples, slabs), vmem(2), vmem(samples, 2),
            vmem(fields, 7), vmem(modes), vmem(modes), vmem(fields, modes),
            vmem(modes), vmem(modes),
            pltpu.SemaphoreType.DMA((sems,)), pltpu.SemaphoreType.DMA((sems,)),
            pltpu.SemaphoreType.DMA((2,)),
        ],
        compiler_params=pltpu.CompilerParams(
            collective_id=0, has_side_effects=True, vmem_limit_bytes=24 << 20
        ),
    )(
        sample_ids,
        index,
        adjoint_source.reshape((modes,) + tile),
        kl_bank.reshape(kl_bank.shape[:2] + tile),
    )
    return state.reshape(adjoint_source.shape), gradient[None]


def on_device(adjoint_source, kl_bank, multi_index, sample_ids):
    slabs, samples = lax.axis_size("space"), lax.axis_size("sample")
    modes, variables = multi_index.shape
    fits = (
        adjoint_source.shape == (1, modes, 1, CELL_ROWS, LANES)
        and slabs == 4
        and CELL_ROWS % samples == 0
        and samples > 1
        and modes % slabs == 0
        and modes == len(basis_rows(variables))
    )
    work = fused_on_device if fits else plain_on_device
    return work(adjoint_source, kl_bank, multi_index, sample_ids)


def solution(mesh):
    return jax.shard_map(
        on_device,
        mesh=mesh,
        in_specs=(
            P(("groups", "sample"), None, "space", None, None),
            P(None, None, "space", None, None),
            P(),
            P(("groups", "sample")),
        ),
        out_specs=(
            P(("groups", "sample"), None, "space", None, None),
            P(("groups", "space"), "sample", None),
        ),
        check_vma=False,
    )
```

```python
import functools
import math
from functools import reduce

import jax
import jax.numpy as jnp
import numpy as np
from jax import lax
from jax.experimental import pallas as pl
from jax.experimental.pallas import tpu as pltpu
from jax.sharding import PartitionSpec as P

ITERS = 2


cross_weight = 1.0 / 64.0


def extended_2(x, sides, width):
    for axis, dim in sides:
        devices, length = (lax.axis_size(axis), x.shape[dim])
        up = [(i, (i + 1) % devices) for i in range(devices - 1)]
        down = [(j, i) for i, j in up]
        last = lax.slice_in_dim(x, length - width, length, axis=dim)
        first = lax.slice_in_dim(x, 0, width, axis=dim)
        before = lax.ppermute(last, axis, up)
        after = lax.ppermute(first, axis, down)
        x = jnp.concatenate([before, x, after], axis=dim)
    return x


def coupling_tables(multi_index):
    upper_rows = multi_index[:, None, :]
    lower_rows = multi_index[None, :, :]
    offset = upper_rows - lower_rows
    distance = jnp.sum(jnp.abs(offset), axis=2)
    larger = jnp.maximum(upper_rows, lower_rows).astype(jnp.float32)
    adjacent = (jnp.abs(offset) == 1) & (distance == 1)[:, :, None]
    raising = jnp.where(adjacent, jnp.sqrt(larger), jnp.zeros_like(larger))
    identity = (distance == 0).astype(jnp.float32)
    coupling = jnp.concatenate([identity[None], jnp.transpose(raising, (2, 0, 1))], axis=0)
    mean_pick = (jnp.sum(multi_index, axis=1) == 0).astype(jnp.float32)
    return (coupling, mean_pick)


def neighbour_views(padded):
    return [
        padded[:, :, 2:, 1:-1, 1:-1],
        padded[:, :, :-2, 1:-1, 1:-1],
        padded[:, :, 1:-1, 2:, 1:-1],
        padded[:, :, 1:-1, :-2, 1:-1],
        padded[:, :, 1:-1, 1:-1, 2:],
        padded[:, :, 1:-1, 1:-1, :-2],
    ]


def face_list(fields, padded):
    weights = [1.0, 1.0, cross_weight, cross_weight, cross_weight, cross_weight]
    return [
        weight * 0.5 * (fields + beside) for weight, beside in zip(weights, neighbour_views(padded))
    ]


def line_prepare(main_band, sub_band, super_band):
    position = lax.broadcasted_iota(jnp.int32, main_band.shape, 1)
    sub_band = jnp.where(position == 0, jnp.zeros_like(sub_band), sub_band)
    super_band = jnp.where(
        position == main_band.shape[1] - 1, jnp.zeros_like(super_band), super_band
    )
    return tuple((jnp.moveaxis(band_arr, 1, 3) for band_arr in (sub_band, main_band, super_band)))


def line_solve(residual, prepared):
    sub_band, main_band, super_band = prepared
    stacked = jnp.transpose(residual, (0, 3, 4, 2, 1))
    solved = lax.linalg.tridiagonal_solve(sub_band, main_band, super_band, stacked)
    return jnp.transpose(solved, (0, 4, 3, 1, 2))


def pad_fields(fields):
    extended = extended_2(fields, (("space", 2),), 1)
    return jnp.pad(extended, ((0, 0), (0, 0), (0, 0), (1, 1), (1, 1)))


def pad_state(field_in):
    extended = extended_2(field_in, (("space", 2),), 1)
    return jnp.pad(extended, ((0, 0), (0, 0), (0, 0), (1, 1), (1, 1)))


def residual_fit(residual, smoothed):
    return lax.psum(jnp.sum(residual * smoothed, axis=(1, 2, 3, 4)), "space")


def spread(values):
    return values[:, None, None, None, None]


def plain_on_device(adjoint_source, kl_bank, multi_index, sample_ids):
    coupling, mean_pick = coupling_tables(multi_index)
    fields = jnp.take(kl_bank, sample_ids, axis=0)
    face_coefs = face_list(fields, pad_fields(fields))
    main_band = reduce(jnp.add, [coef[:, 0] for coef in face_coefs])
    sub_band = -face_coefs[1][:, 0]
    super_band = -face_coefs[0][:, 0]
    main_band, sub_band, super_band = (
        lax.all_to_all(main_band, "space", split_axis=3, concat_axis=1, tiled=True),
        lax.all_to_all(sub_band, "space", split_axis=3, concat_axis=1, tiled=True),
        lax.all_to_all(super_band, "space", split_axis=3, concat_axis=1, tiled=True),
    )
    prepared = line_prepare(main_band, sub_band, super_band)

    def precondition(residual):
        line_data = lax.all_to_all(residual, "space", split_axis=4, concat_axis=2, tiled=True)
        solved = line_solve(line_data, prepared)
        return lax.all_to_all(solved, "space", split_axis=2, concat_axis=4, tiled=True)

    def operate(field_in):
        views = neighbour_views(pad_state(field_in))
        weighted = reduce(
            jnp.add,
            [
                coef[:, :, None] * (field_in[:, None] - beside[:, None])
                for coef, beside in zip(face_coefs, views)
            ],
        )
        return jnp.einsum(
            "kij,skjxyz->sixyz",
            coupling,
            weighted,
            precision=lax.Precision.HIGHEST,
            preferred_element_type=jnp.float32,
        )

    solution = jnp.zeros_like(adjoint_source)
    residual = adjoint_source
    smoothed = precondition(residual)
    direction = smoothed
    fit_now = residual_fit(residual, smoothed)
    for iteration in range(ITERS):
        image_vec = operate(direction)
        curvature_sum = lax.psum(jnp.sum(direction * image_vec, axis=(1, 2, 3, 4)), "space")
        step_size = fit_now / curvature_sum
        solution = solution + spread(step_size) * direction
        residual = residual - spread(step_size) * image_vec
        if iteration + 1 < ITERS:
            smoothed = precondition(residual)
            fit_next = residual_fit(residual, smoothed)
            direction = smoothed + spread(fit_next / fit_now) * direction
            fit_now = fit_next
    sample_count = solution.shape[0] * lax.axis_size("sample")
    mean_term = (
        jnp.einsum(
            "p,spxyz->xyz",
            mean_pick,
            solution,
            precision=lax.Precision.HIGHEST,
            preferred_element_type=jnp.float32,
        )
        / sample_count
    )
    gradient = lax.psum_scatter(mean_term, "sample", scatter_dimension=1, tiled=True)
    return (solution, gradient)


DEGREE = 3
CELL_ROWS = 8
LANES = 128


def basis_rows(variables):
    rows = [[]]
    for _ in range(variables):
        rows = [row + [d] for row in rows for d in range(DEGREE + 1) if sum(row) + d <= DEGREE]
    return rows


def couplings(variables):
    rows = basis_rows(variables)
    place = {tuple(row): i for i, row in enumerate(rows)}
    result = []
    for row in rows:
        mine = []
        for k in range(variables):
            for change in (-1, 1):
                other = list(row)
                other[k] += change
                j = place.get(tuple(other))
                if j is not None:
                    mine.append((k + 1, j, math.sqrt(max(row[k], other[k]))))
        result.append(mine)
    return rows, result


def roll(x, shift, axis=1):
    shift %= x.shape[axis]
    return x if shift == 0 else pltpu.roll(x, shift, axis)


def kernel(
    slabs, samples, variables,
    sid_ref, idx_ref, src_hbm, kl_hbm,
    out_ref, grad_ref,
    src_ref, kl_ref, f_send, f_recv, r_send, r_recv, zx_send, zx_recv, ux_send, ux_recv,
    halo_send, halo_recv, sum_send, sum_recv, mean_send, mean_recv,
    coefs, z_vec, u_vec, terms, zx_vec, ux_vec,
    send_sem, recv_sem, load_sem,
):
    rows, links = couplings(variables)
    modes = len(rows)
    mean_mode = rows.index([0] * variables)
    fields = variables + 1
    width = LANES // slabs
    me = lax.axis_index("space")
    mine = lax.axis_index("sample")

    lane = lax.broadcasted_iota(jnp.int32, (CELL_ROWS, LANES), 1)
    row = lax.broadcasted_iota(jnp.int32, (CELL_ROWS, LANES), 0)
    block = lane // width
    inner = lane % width
    is_block = [block == b for b in range(slabs)]
    low_edge, high_edge = inner == 0, inner == width - 1
    zero = jnp.zeros((CELL_ROWS, LANES), jnp.float32)

    def pack(values, dest):
        result = zero
        for j, value in enumerate(values):
            result = jnp.where(is_block[j], roll(value, (j - dest) * width), result)
        return result

    def unpack(values, j):
        result = zero
        for b, value in enumerate(values):
            result = jnp.where(is_block[b], roll(value, (b - j) * width), result)
        return result

    def exchange(send, recv, first, low=0, high=None):
        piece = pl.ds(low, (send.shape[1] if high is None else high) - low)
        copies = []
        for away in range(1, slabs):
            dest = lax.rem(me + away, slabs)
            copies.append(
                pltpu.make_async_remote_copy(
                    src_ref=send.at[dest, piece],
                    dst_ref=recv.at[me, piece],
                    send_sem=send_sem.at[first + away - 1],
                    recv_sem=recv_sem.at[first + away - 1],
                    device_id={"space": dest},
                    device_id_type=pl.DeviceIdType.MESH,
                )
            )
        return copies

    loads = [
        pltpu.make_async_copy(kl_hbm, kl_ref, load_sem.at[0]),
        pltpu.make_async_copy(src_hbm, src_ref, load_sem.at[1]),
    ]
    for load in loads:
        load.start()
    halo_recv[...] = jnp.zeros_like(halo_recv)
    barrier = pltpu.get_barrier_semaphore()
    others = [(x, y) for x in range(samples) for y in range(slabs) if x or y]
    peers = [(lax.rem(mine + x, samples), lax.rem(me + y, slabs)) for x, y in others]
    for sample, slab in peers:
        pl.semaphore_signal(
            barrier, inc=1, device_id={"sample": sample, "space": slab},
            device_id_type=pl.DeviceIdType.MESH,
        )

    loads[0].wait()
    sid = sid_ref[0]
    chunks = [kl_ref[sid, k] for k in range(fields)]
    chunks = (
        chunks
        + [jnp.where(lane == LANES - 1, 0.0, roll(f, -1)) for f in chunks]
        + [jnp.where(lane == 0, 0.0, roll(f, 1)) for f in chunks]
    )
    for p in range(f_send.shape[1]):
        group = chunks[p * slabs:(p + 1) * slabs]
        for dest in range(slabs):
            f_send[dest, p] = pack(group, dest)
    f_recv[me] = f_send[me]

    pl.semaphore_wait(barrier, len(peers))
    f_copies = exchange(f_send, f_recv, 0)
    for copy in f_copies:
        copy.start()

    groups = modes // slabs
    def pack_all(load, send, low, high):
        for q in range(low, high, 4):
            batch = range(q, min(high, q + 4))
            values = [[load(p * slabs + j) for j in range(slabs)] for p in batch]
            packed = [[pack(group, dest) for dest in range(slabs)] for group in values]
            for p, row_packed in zip(batch, packed):
                for dest in range(slabs):
                    send[dest, p] = row_packed[dest]
        return send[me, pl.ds(low, high - low)]

    def unpack_all(recv, vec):
        for q in range(0, groups, 4):
            batch = range(q, min(groups, q + 4))
            values = [[recv[b, p] for b in range(slabs)] for p in batch]
            values = [unpack(group, j) for group in values for j in range(slabs)]
            for n, value in enumerate(values):
                vec[q * slabs + n] = value

    loads[1].wait()
    first = 4 * (slabs - 1) + 4 + len(peers) + samples - 1
    halves = [(0, groups // 2), (groups // 2, groups)]
    r_copies = []
    for n, (low, high) in enumerate(halves):
        r_recv[me, pl.ds(low, high - low)] = pack_all(
            lambda m: src_ref[idx_ref[m]], r_send, low, high
        )
        r_copies.append(exchange(r_send, r_recv, first + n * (slabs - 1), low, high))
        for copy in r_copies[-1]:
            copy.start()

    for copy in f_copies:
        copy.wait()

    def field(number):
        p, j = divmod(number, slabs)
        return unpack([f_recv[b, p] for b in range(slabs)], j)

    lowest = low_edge & (me == 0)
    highest = high_edge & (me == slabs - 1)
    mean_diag = mean_next = None
    for k in range(fields):
        f = field(k)
        xp = 0.5 * (f + jnp.where(is_block[slabs - 1], 0.0, roll(f, -width)))
        xm = 0.5 * (f + jnp.where(is_block[0], 0.0, roll(f, width)))
        half = 0.5 * cross_weight
        yp = half * (f + jnp.where(row == CELL_ROWS - 1, 0.0, roll(f, -1, 0)))
        ym = half * (f + jnp.where(row == 0, 0.0, roll(f, 1, 0)))
        zp = half * (f + field(fields + k))
        zm = half * (f + field(2 * fields + k))
        diag = xp + xm + yp + ym + zp + zm
        if k == 0:
            mean_diag, mean_next = diag, xp
        coefs[k, 0] = diag
        coefs[k, 1] = jnp.where(is_block[slabs - 1], 0.0, xp)
        coefs[k, 2] = jnp.where(is_block[0], 0.0, xm)
        coefs[k, 3] = jnp.where(row == CELL_ROWS - 1, 0.0, yp)
        coefs[k, 4] = jnp.where(row == 0, 0.0, ym)
        coefs[k, 5] = jnp.where(highest, 0.0, zp)
        coefs[k, 6] = jnp.where(lowest, 0.0, zm)

    d = [unpack([mean_diag] * slabs, x) for x in range(slabs)]
    a = [unpack([mean_next] * slabs, x) for x in range(slabs - 1)]
    one = jnp.ones_like(zero)
    lead = [one, d[0]]
    for x in range(1, slabs):
        lead.append(d[x] * lead[x] - a[x - 1] * a[x - 1] * lead[x - 1])
    trail = [one, d[slabs - 1]]
    for x in range(slabs - 2, -1, -1):
        trail.append(d[x] * trail[-1] - a[x] * a[x] * trail[-2])
    trail = trail[::-1]
    scale = one / lead[slabs]
    inverse = {}
    for i in range(slabs):
        between = scale
        for j in range(i, slabs):
            if j > i:
                between = between * a[j - 1]
            inverse[i, j] = inverse[j, i] = between * lead[i] * trail[j + 1]
    line = []
    for shift in range(slabs):
        weight = zero
        for x in range(slabs):
            weight = jnp.where(is_block[x], inverse[x, (x - shift) % slabs], weight)
        line.append(weight)

    def line_inverse(value):
        result = line[0] * value
        for shift in range(1, slabs):
            result = result + line[shift] * roll(value, shift * width)
        return result

    def send_halo(vec, number):
        packs = halo_send.shape[2]
        for p in range(packs):
            up = down = zero
            for m in range(p * width, min(modes, (p + 1) * width)):
                spot = m % width
                value = vec[m]
                up = jnp.where(inner == spot, roll(value, spot - (width - 1)), up)
                down = jnp.where(inner == spot, roll(value, spot), down)
            halo_send[number, 0, p] = up
            halo_send[number, 1, p] = down
        first = 2 * (slabs - 1) + 2 * number
        copies = []
        for way, step in ((0, 1), (1, slabs - 1)):
            copies.append(
                pltpu.make_async_remote_copy(
                    src_ref=halo_send.at[number, way],
                    dst_ref=halo_recv.at[number, way],
                    send_sem=send_sem.at[first + way],
                    recv_sem=recv_sem.at[first + way],
                    device_id={"space": lax.rem(me + step, slabs)},
                    device_id_type=pl.DeviceIdType.MESH,
                )
            )
        up, down = copies

        @pl.when(me < slabs - 1)
        def _():
            up.start()

        @pl.when(me > 0)
        def _():
            down.start()

        return up, down

    def wait_halo(copies):
        up, down = copies

        @pl.when(me < slabs - 1)
        def _():
            up.wait_send()
            down.wait_recv()

        @pl.when(me > 0)
        def _():
            down.wait_send()
            up.wait_recv()

    needed = [set() for _ in range(modes)]
    for i in range(modes):
        for k, j, _ in links[i]:
            needed[j].add(k)

    def rest_terms(vec, number):
        for q in range(0, modes, 4):
            batch = range(q, min(modes, q + 4))
            values = [vec[m] for m in batch]
            sides = []
            for m, value in zip(batch, values):
                p, spot = divmod(m, width)
                above = roll(halo_recv[number, 1, p], width - 1 - spot)
                below = roll(halo_recv[number, 0, p], -spot)
                sides.append([
                    roll(value, -width), roll(value, width), roll(value, -1, 0), roll(value, 1, 0),
                    jnp.where(high_edge, above, roll(value, -1)),
                    jnp.where(low_edge, below, roll(value, 1)),
                ])
            results = {}
            for k in range(fields):
                factor = [coefs[k, n] for n in range(7)]
                for m, value, beside in zip(batch, values, sides):
                    if k == 0:
                        results[k, m] = -(
                            (factor[3] * beside[2] + factor[4] * beside[3])
                            + (factor[5] * beside[4] + factor[6] * beside[5])
                        )
                    elif k in needed[m]:
                        parts = [factor[1 + face] * beside[face] for face in range(6)]
                        results[k, m] = factor[0] * value - (
                            (parts[0] + parts[1]) + (parts[2] + parts[3]) + (parts[4] + parts[5])
                        )
            for (k, m), result in results.items():
                terms[k, m] = result

    def coupled(i):
        total = terms[0, i]
        by_weight = {}
        for k, j, weight in links[i]:
            by_weight.setdefault(weight, []).append((k, j))
        for weight, pairs in by_weight.items():
            part = terms[pairs[0][0], pairs[0][1]]
            for k, j in pairs[1:]:
                part = part + terms[k, j]
            total = total + (part if weight == 1.0 else np.float32(weight) * part)
        return total

    fit = zero
    for (low, high), copies in zip(halves, r_copies):
        for copy in copies:
            copy.wait()
        for q in range(low, high, 4):
            batch = range(q, min(high, q + 4))
            values = [[r_recv[b, p] for b in range(slabs)] for p in batch]
            residuals = [unpack(group, j) for group in values for j in range(slabs)]
            results = [line_inverse(residual) for residual in residuals]
            for n, (residual, smoothed) in enumerate(zip(residuals, results)):
                z_vec[q * slabs + n] = smoothed
                fit = fit + residual * smoothed
    copies = send_halo(z_vec, 0)
    first = 2 * (slabs - 1) + 4
    zx_recv[me] = pack_all(lambda m: z_vec[m], zx_send, 0, groups)
    zx_copies = exchange(zx_send, zx_recv, first)
    for copy in zx_copies:
        copy.start()
    wait_halo(copies)
    rest_terms(z_vec, 0)
    cross = square = zero
    for q in range(0, modes, 8):
        batch = range(q, min(modes, q + 8))
        rests = [coupled(i) for i in batch]
        results = [line_inverse(rest) for rest in rests]
        for i, rest, smoothed in zip(batch, rests, results):
            u_vec[i] = smoothed
            cross = cross + z_vec[i] * rest
            square = square + rest * smoothed
    copies = send_halo(u_vec, 1)
    first += slabs - 1
    ux_recv[me] = pack_all(lambda m: u_vec[m], ux_send, 0, groups)
    ux_copies = exchange(ux_send, ux_recv, first)
    for copy in ux_copies:
        copy.start()
    wait_halo(copies)
    rest_terms(u_vec, 1)
    last = [zero] * 4
    for i in range(modes):
        last[i % 4] = last[i % 4] + u_vec[i] * coupled(i)
    last = (last[0] + last[1]) + (last[2] + last[3])

    sums = zero
    for number, value in enumerate((fit, cross, square, last)):
        sums = jnp.where(row == number, jnp.sum(value, axis=0, keepdims=True), sums)
    sum_send[...] = sums
    first += slabs - 1
    sum_copies = []
    for n, (sample, slab) in enumerate(peers):
        sum_copies.append(
            pltpu.make_async_remote_copy(
                src_ref=sum_send,
                dst_ref=sum_recv.at[mine, me],
                send_sem=send_sem.at[first + n],
                recv_sem=recv_sem.at[first + n],
                device_id={"sample": sample, "space": slab},
                device_id_type=pl.DeviceIdType.MESH,
            )
        )
    for copy in sum_copies:
        copy.start()
    sum_recv[mine, me] = sums

    for copy in zx_copies:
        copy.wait()
    unpack_all(zx_recv, zx_vec)
    for copy in ux_copies:
        copy.wait()
    p, j = divmod(mean_mode, slabs)
    mean_send[0] = zx_vec[mean_mode]
    mean_send[1] = unpack([ux_recv[b, p] for b in range(slabs)], j)
    first += len(peers)
    mean_copies = []
    for away in range(1, samples):
        mean_copies.append(
            pltpu.make_async_remote_copy(
                src_ref=mean_send,
                dst_ref=mean_recv.at[mine],
                send_sem=send_sem.at[first + away - 1],
                recv_sem=recv_sem.at[first + away - 1],
                device_id={"sample": lax.rem(mine + away, samples)},
                device_id_type=pl.DeviceIdType.MESH,
            )
        )
    for copy in mean_copies:
        copy.start()
    mean_recv[mine] = mean_send[...]
    unpack_all(ux_recv, ux_vec)
    for copy in sum_copies[:slabs - 1]:
        copy.wait()

    def parts(sample):
        total = reduce(jnp.add, [sum_recv[sample, b] for b in range(slabs)])
        total = jnp.sum(total, axis=1, keepdims=True)
        f, e, g, h = (jnp.broadcast_to(total[n:n + 1], zero.shape) for n in range(4))
        curve = f + e
        step = f / curve
        ratio = (f * g - e * e) / (curve * curve)
        z_part = e / curve + ratio
        curve_next = (
            z_part * z_part * curve - 2.0 * z_part * step * (e + g) + step * step * (g + h)
        )
        step_next = ratio * f / curve_next
        return step + step_next * z_part, -step_next * step

    z_part, u_part = parts(mine)
    stores = []
    for q in range(0, modes, 8):
        batch = range(q, min(modes, q + 8))
        places = [idx_ref[modes + i] for i in batch]
        results = [z_part * zx_vec[place] + u_part * ux_vec[place] for place in places]
        for i, result in zip(batch, results):
            src_ref[i] = result
        rows_now = pl.ds(q, len(batch))
        stores.append(
            pltpu.make_async_copy(
                src_ref.at[rows_now], out_ref.at[rows_now], load_sem.at[2 + q // 8]
            )
        )
        stores[-1].start()
    for copy in sum_copies[slabs - 1:] + mean_copies:
        copy.wait()
    total = zero
    for sample in range(samples):
        z_part, u_part = parts(sample)
        total = total + (z_part * mean_recv[sample, 0] + u_part * mean_recv[sample, 1])
    total = total * (1.0 / samples)
    share = CELL_ROWS // samples
    result = total[0:share]
    for b in range(1, samples):
        result = jnp.where(mine == b, total[b * share:(b + 1) * share], result)
    grad_ref[...] = result
    for store in stores:
        store.wait()


def fused_on_device(adjoint_source, kl_bank, multi_index, sample_ids):
    slabs, samples = lax.axis_size("space"), lax.axis_size("sample")
    modes, variables = multi_index.shape
    fields = variables + 1
    code = reduce(lambda c, k: c * (DEGREE + 1) + multi_index[:, k], range(variables), 0)
    numbers = jnp.arange(modes, dtype=jnp.int32)
    rank = jnp.sum((code[None, :] < code[:, None]).astype(jnp.int32), axis=1)
    source = jnp.sum(jnp.where(rank[None, :] == numbers[:, None], numbers[None, :], 0), axis=1)
    index = jnp.concatenate([source, rank])
    tile = (CELL_ROWS, LANES)
    groups = modes // slabs
    f_groups = -(-3 * fields // slabs)
    halos = -(-modes // (LANES // slabs))
    vmem = lambda *shape: pltpu.VMEM(shape + tile, jnp.float32)
    sems = 6 * (slabs - 1) + 4 + slabs * samples - 1 + samples - 1
    in_vmem = pl.BlockSpec(memory_space=pltpu.VMEM)
    in_hbm = pl.BlockSpec(memory_space=pltpu.HBM)
    in_smem = pl.BlockSpec(memory_space=pltpu.SMEM)
    state, gradient = pl.pallas_call(
        functools.partial(kernel, slabs, samples, variables),
        out_shape=(
            jax.ShapeDtypeStruct((modes,) + tile, jnp.float32),
            jax.ShapeDtypeStruct((CELL_ROWS // samples, LANES), jnp.float32),
        ),
        in_specs=[in_smem, in_smem, in_hbm, in_hbm],
        out_specs=(in_hbm, in_vmem),
        scratch_shapes=[
            vmem(modes), vmem(*kl_bank.shape[:2]),
            vmem(slabs, f_groups), vmem(slabs, f_groups),
            vmem(slabs, groups), vmem(slabs, groups),
            vmem(slabs, groups), vmem(slabs, groups),
            vmem(slabs, groups), vmem(slabs, groups),
            vmem(2, 2, halos), vmem(2, 2, halos),
            vmem(), vmem(samples, slabs), vmem(2), vmem(samples, 2),
            vmem(fields, 7), vmem(modes), vmem(modes), vmem(fields, modes),
            vmem(modes), vmem(modes),
            pltpu.SemaphoreType.DMA((sems,)), pltpu.SemaphoreType.DMA((sems,)),
            pltpu.SemaphoreType.DMA((2 + -(-modes // 8),)),
        ],
        compiler_params=pltpu.CompilerParams(
            collective_id=0, has_side_effects=True, vmem_limit_bytes=60 << 20
        ),
    )(
        sample_ids,
        index,
        adjoint_source.reshape((modes,) + tile),
        kl_bank.reshape(kl_bank.shape[:2] + tile),
    )
    return state.reshape(adjoint_source.shape), gradient[None]


def on_device(adjoint_source, kl_bank, multi_index, sample_ids):
    slabs, samples = lax.axis_size("space"), lax.axis_size("sample")
    modes, variables = multi_index.shape
    fits = (
        adjoint_source.shape == (1, modes, 1, CELL_ROWS, LANES)
        and slabs == 4
        and CELL_ROWS % samples == 0
        and samples > 1
        and modes % slabs == 0
        and modes == len(basis_rows(variables))
    )
    work = fused_on_device if fits else plain_on_device
    return work(adjoint_source, kl_bank, multi_index, sample_ids)


def solution(mesh):
    return jax.shard_map(
        on_device,
        mesh=mesh,
        in_specs=(
            P(("groups", "sample"), None, "space", None, None),
            P(None, None, "space", None, None),
            P(),
            P(("groups", "sample")),
        ),
        out_specs=(
            P(("groups", "sample"), None, "space", None, None),
            P(("groups", "space"), "sample", None),
        ),
        check_vma=False,
    )
```

```python
import functools
import math
from functools import reduce

import jax
import jax.numpy as jnp
import numpy as np
from jax import lax
from jax.experimental import pallas as pl
from jax.experimental.pallas import tpu as pltpu
from jax.sharding import PartitionSpec as P

ITERS = 2


cross_weight = 1.0 / 64.0


def extended_2(x, sides, width):
    for axis, dim in sides:
        devices, length = (lax.axis_size(axis), x.shape[dim])
        up = [(i, (i + 1) % devices) for i in range(devices - 1)]
        down = [(j, i) for i, j in up]
        last = lax.slice_in_dim(x, length - width, length, axis=dim)
        first = lax.slice_in_dim(x, 0, width, axis=dim)
        before = lax.ppermute(last, axis, up)
        after = lax.ppermute(first, axis, down)
        x = jnp.concatenate([before, x, after], axis=dim)
    return x


def coupling_tables(multi_index):
    upper_rows = multi_index[:, None, :]
    lower_rows = multi_index[None, :, :]
    offset = upper_rows - lower_rows
    distance = jnp.sum(jnp.abs(offset), axis=2)
    larger = jnp.maximum(upper_rows, lower_rows).astype(jnp.float32)
    adjacent = (jnp.abs(offset) == 1) & (distance == 1)[:, :, None]
    raising = jnp.where(adjacent, jnp.sqrt(larger), jnp.zeros_like(larger))
    identity = (distance == 0).astype(jnp.float32)
    coupling = jnp.concatenate([identity[None], jnp.transpose(raising, (2, 0, 1))], axis=0)
    mean_pick = (jnp.sum(multi_index, axis=1) == 0).astype(jnp.float32)
    return (coupling, mean_pick)


def neighbour_views(padded):
    return [
        padded[:, :, 2:, 1:-1, 1:-1],
        padded[:, :, :-2, 1:-1, 1:-1],
        padded[:, :, 1:-1, 2:, 1:-1],
        padded[:, :, 1:-1, :-2, 1:-1],
        padded[:, :, 1:-1, 1:-1, 2:],
        padded[:, :, 1:-1, 1:-1, :-2],
    ]


def face_list(fields, padded):
    weights = [1.0, 1.0, cross_weight, cross_weight, cross_weight, cross_weight]
    return [
        weight * 0.5 * (fields + beside) for weight, beside in zip(weights, neighbour_views(padded))
    ]


def line_prepare(main_band, sub_band, super_band):
    position = lax.broadcasted_iota(jnp.int32, main_band.shape, 1)
    sub_band = jnp.where(position == 0, jnp.zeros_like(sub_band), sub_band)
    super_band = jnp.where(
        position == main_band.shape[1] - 1, jnp.zeros_like(super_band), super_band
    )
    return tuple((jnp.moveaxis(band_arr, 1, 3) for band_arr in (sub_band, main_band, super_band)))


def line_solve(residual, prepared):
    sub_band, main_band, super_band = prepared
    stacked = jnp.transpose(residual, (0, 3, 4, 2, 1))
    solved = lax.linalg.tridiagonal_solve(sub_band, main_band, super_band, stacked)
    return jnp.transpose(solved, (0, 4, 3, 1, 2))


def pad_fields(fields):
    extended = extended_2(fields, (("space", 2),), 1)
    return jnp.pad(extended, ((0, 0), (0, 0), (0, 0), (1, 1), (1, 1)))


def pad_state(field_in):
    extended = extended_2(field_in, (("space", 2),), 1)
    return jnp.pad(extended, ((0, 0), (0, 0), (0, 0), (1, 1), (1, 1)))


def residual_fit(residual, smoothed):
    return lax.psum(jnp.sum(residual * smoothed, axis=(1, 2, 3, 4)), "space")


def spread(values):
    return values[:, None, None, None, None]


def plain_on_device(adjoint_source, kl_bank, multi_index, sample_ids):
    coupling, mean_pick = coupling_tables(multi_index)
    fields = jnp.take(kl_bank, sample_ids, axis=0)
    face_coefs = face_list(fields, pad_fields(fields))
    main_band = reduce(jnp.add, [coef[:, 0] for coef in face_coefs])
    sub_band = -face_coefs[1][:, 0]
    super_band = -face_coefs[0][:, 0]
    main_band, sub_band, super_band = (
        lax.all_to_all(main_band, "space", split_axis=3, concat_axis=1, tiled=True),
        lax.all_to_all(sub_band, "space", split_axis=3, concat_axis=1, tiled=True),
        lax.all_to_all(super_band, "space", split_axis=3, concat_axis=1, tiled=True),
    )
    prepared = line_prepare(main_band, sub_band, super_band)

    def precondition(residual):
        line_data = lax.all_to_all(residual, "space", split_axis=4, concat_axis=2, tiled=True)
        solved = line_solve(line_data, prepared)
        return lax.all_to_all(solved, "space", split_axis=2, concat_axis=4, tiled=True)

    def operate(field_in):
        views = neighbour_views(pad_state(field_in))
        weighted = reduce(
            jnp.add,
            [
                coef[:, :, None] * (field_in[:, None] - beside[:, None])
                for coef, beside in zip(face_coefs, views)
            ],
        )
        return jnp.einsum(
            "kij,skjxyz->sixyz",
            coupling,
            weighted,
            precision=lax.Precision.HIGHEST,
            preferred_element_type=jnp.float32,
        )

    solution = jnp.zeros_like(adjoint_source)
    residual = adjoint_source
    smoothed = precondition(residual)
    direction = smoothed
    fit_now = residual_fit(residual, smoothed)
    for iteration in range(ITERS):
        image_vec = operate(direction)
        curvature_sum = lax.psum(jnp.sum(direction * image_vec, axis=(1, 2, 3, 4)), "space")
        step_size = fit_now / curvature_sum
        solution = solution + spread(step_size) * direction
        residual = residual - spread(step_size) * image_vec
        if iteration + 1 < ITERS:
            smoothed = precondition(residual)
            fit_next = residual_fit(residual, smoothed)
            direction = smoothed + spread(fit_next / fit_now) * direction
            fit_now = fit_next
    sample_count = solution.shape[0] * lax.axis_size("sample")
    mean_term = (
        jnp.einsum(
            "p,spxyz->xyz",
            mean_pick,
            solution,
            precision=lax.Precision.HIGHEST,
            preferred_element_type=jnp.float32,
        )
        / sample_count
    )
    gradient = lax.psum_scatter(mean_term, "sample", scatter_dimension=1, tiled=True)
    return (solution, gradient)


DEGREE = 3
CELL_ROWS = 8
LANES = 128


def basis_rows(variables):
    rows = [[]]
    for _ in range(variables):
        rows = [row + [d] for row in rows for d in range(DEGREE + 1) if sum(row) + d <= DEGREE]
    return rows


def couplings(variables):
    rows = basis_rows(variables)
    place = {tuple(row): i for i, row in enumerate(rows)}
    result = []
    for row in rows:
        mine = []
        for k in range(variables):
            for change in (-1, 1):
                other = list(row)
                other[k] += change
                j = place.get(tuple(other))
                if j is not None:
                    mine.append((k + 1, j, math.sqrt(max(row[k], other[k]))))
        result.append(mine)
    return rows, result


def roll(x, shift, axis=1):
    shift %= x.shape[axis]
    return x if shift == 0 else pltpu.roll(x, shift, axis)


def kernel(
    slabs, samples, variables,
    sid_ref, idx_ref, src_hbm, kl_hbm,
    out_ref, grad_ref,
    src_ref, kl_ref, f_send, f_recv, r_send, r_recv, zx_send, zx_recv, ux_send, ux_recv,
    halo_send, halo_recv, sum_send, sum_recv, mean_send, mean_recv,
    coefs, z_vec, u_vec, terms, zx_vec, ux_vec,
    send_sem, recv_sem, load_sem,
):
    rows, links = couplings(variables)
    modes = len(rows)
    mean_mode = rows.index([0] * variables)
    fields = variables + 1
    width = LANES // slabs
    me = lax.axis_index("space")
    mine = lax.axis_index("sample")

    lane = lax.broadcasted_iota(jnp.int32, (CELL_ROWS, LANES), 1)
    row = lax.broadcasted_iota(jnp.int32, (CELL_ROWS, LANES), 0)
    block = lane // width
    inner = lane % width
    is_block = [block == b for b in range(slabs)]
    low_edge, high_edge = inner == 0, inner == width - 1
    zero = jnp.zeros((CELL_ROWS, LANES), jnp.float32)

    def pack(values, dest):
        result = zero
        for j, value in enumerate(values):
            result = jnp.where(is_block[j], roll(value, (j - dest) * width), result)
        return result

    def unpack(values, j):
        result = zero
        for b, value in enumerate(values):
            result = jnp.where(is_block[b], roll(value, (b - j) * width), result)
        return result

    def exchange(send, recv, first, low=0, high=None):
        piece = pl.ds(low, (send.shape[1] if high is None else high) - low)
        copies = []
        for away in range(1, slabs):
            dest = lax.rem(me + away, slabs)
            copies.append(
                pltpu.make_async_remote_copy(
                    src_ref=send.at[dest, piece],
                    dst_ref=recv.at[me, piece],
                    send_sem=send_sem.at[first + away - 1],
                    recv_sem=recv_sem.at[first + away - 1],
                    device_id={"space": dest},
                    device_id_type=pl.DeviceIdType.MESH,
                )
            )
        return copies

    loads = [
        pltpu.make_async_copy(kl_hbm, kl_ref, load_sem.at[0]),
        pltpu.make_async_copy(src_hbm, src_ref, load_sem.at[1]),
    ]
    for load in loads:
        load.start()
    halo_recv[...] = jnp.zeros_like(halo_recv)
    barrier = pltpu.get_barrier_semaphore()
    others = [(x, y) for x in range(samples) for y in range(slabs) if x or y]
    peers = [(lax.rem(mine + x, samples), lax.rem(me + y, slabs)) for x, y in others]
    for sample, slab in peers:
        pl.semaphore_signal(
            barrier, inc=1, device_id={"sample": sample, "space": slab},
            device_id_type=pl.DeviceIdType.MESH,
        )

    loads[0].wait()
    sid = sid_ref[0]
    chunks = [kl_ref[sid, k] for k in range(fields)]
    for dest in range(slabs):
        f_send[dest, 0] = pack(chunks[:slabs], dest)
        second = pack(chunks[slabs:], dest)
        for k, f in enumerate(chunks):
            if dest < slabs - 1:
                spot = (slabs - 2) * width + k
                second = jnp.where(lane == spot, roll(f, spot - (dest + 1) * width), second)
            if dest > 0:
                spot = (slabs - 1) * width + k
                second = jnp.where(lane == spot, roll(f, spot - dest * width + 1), second)
        f_send[dest, 1] = second
    f_recv[me] = f_send[me]

    pl.semaphore_wait(barrier, len(peers))
    f_copies = exchange(f_send, f_recv, 0)
    for copy in f_copies:
        copy.start()

    groups = modes // slabs
    def pack_all(load, send, low, high):
        for q in range(low, high, 4):
            batch = range(q, min(high, q + 4))
            values = [[load(p * slabs + j) for j in range(slabs)] for p in batch]
            packed = [[pack(group, dest) for dest in range(slabs)] for group in values]
            for p, row_packed in zip(batch, packed):
                for dest in range(slabs):
                    send[dest, p] = row_packed[dest]
        return send[me, pl.ds(low, high - low)]

    def unpack_all(recv, vec):
        for q in range(0, groups, 4):
            batch = range(q, min(groups, q + 4))
            values = [[recv[b, p] for b in range(slabs)] for p in batch]
            values = [unpack(group, j) for group in values for j in range(slabs)]
            for n, value in enumerate(values):
                vec[q * slabs + n] = value

    loads[1].wait()
    first = 4 * (slabs - 1) + 4 + len(peers) + samples - 1
    halves = [(0, groups // 2), (groups // 2, groups)]
    r_copies = []
    for n, (low, high) in enumerate(halves):
        r_recv[me, pl.ds(low, high - low)] = pack_all(
            lambda m: src_ref[idx_ref[m]], r_send, low, high
        )
        r_copies.append(exchange(r_send, r_recv, first + n * (slabs - 1), low, high))
        for copy in r_copies[-1]:
            copy.start()

    for copy in f_copies:
        copy.wait()

    def field(number):
        p, j = divmod(number, slabs)
        return unpack([f_recv[b, p] for b in range(slabs)], j)

    lowest = low_edge & (me == 0)
    highest = high_edge & (me == slabs - 1)
    mean_diag = mean_next = None
    for k in range(fields):
        f = field(k)
        xp = 0.5 * (f + jnp.where(is_block[slabs - 1], 0.0, roll(f, -width)))
        xm = 0.5 * (f + jnp.where(is_block[0], 0.0, roll(f, width)))
        half = 0.5 * cross_weight
        yp = half * (f + jnp.where(row == CELL_ROWS - 1, 0.0, roll(f, -1, 0)))
        ym = half * (f + jnp.where(row == 0, 0.0, roll(f, 1, 0)))
        above = below = zero
        for b in range(slabs):
            edges = f_recv[b, 1]
            spot = b * width + width - 1
            above = jnp.where(lane == spot, roll(edges, spot - (slabs - 2) * width - k), above)
            spot = b * width
            below = jnp.where(lane == spot, roll(edges, spot - (slabs - 1) * width - k), below)
        zp = half * (f + jnp.where(high_edge, above, roll(f, -1)))
        zm = half * (f + jnp.where(low_edge, below, roll(f, 1)))
        diag = xp + xm + yp + ym + zp + zm
        if k == 0:
            mean_diag, mean_next = diag, xp
        coefs[k, 0] = diag
        coefs[k, 1] = jnp.where(is_block[slabs - 1], 0.0, xp)
        coefs[k, 2] = jnp.where(is_block[0], 0.0, xm)
        coefs[k, 3] = jnp.where(row == CELL_ROWS - 1, 0.0, yp)
        coefs[k, 4] = jnp.where(row == 0, 0.0, ym)
        coefs[k, 5] = jnp.where(highest, 0.0, zp)
        coefs[k, 6] = jnp.where(lowest, 0.0, zm)

    d = [unpack([mean_diag] * slabs, x) for x in range(slabs)]
    a = [unpack([mean_next] * slabs, x) for x in range(slabs - 1)]
    one = jnp.ones_like(zero)
    lead = [one, d[0]]
    for x in range(1, slabs):
        lead.append(d[x] * lead[x] - a[x - 1] * a[x - 1] * lead[x - 1])
    trail = [one, d[slabs - 1]]
    for x in range(slabs - 2, -1, -1):
        trail.append(d[x] * trail[-1] - a[x] * a[x] * trail[-2])
    trail = trail[::-1]
    scale = one / lead[slabs]
    inverse = {}
    for i in range(slabs):
        between = scale
        for j in range(i, slabs):
            if j > i:
                between = between * a[j - 1]
            inverse[i, j] = inverse[j, i] = between * lead[i] * trail[j + 1]
    line = []
    for shift in range(slabs):
        weight = zero
        for x in range(slabs):
            weight = jnp.where(is_block[x], inverse[x, (x - shift) % slabs], weight)
        line.append(weight)

    def line_inverse(value):
        result = line[0] * value
        for shift in range(1, slabs):
            result = result + line[shift] * roll(value, shift * width)
        return result

    def send_halo(vec, number):
        packs = halo_send.shape[2]
        for p in range(packs):
            up = down = zero
            for m in range(p * width, min(modes, (p + 1) * width)):
                spot = m % width
                value = vec[m]
                up = jnp.where(inner == spot, roll(value, spot - (width - 1)), up)
                down = jnp.where(inner == spot, roll(value, spot), down)
            halo_send[number, 0, p] = up
            halo_send[number, 1, p] = down
        first = 2 * (slabs - 1) + 2 * number
        copies = []
        for way, step in ((0, 1), (1, slabs - 1)):
            copies.append(
                pltpu.make_async_remote_copy(
                    src_ref=halo_send.at[number, way],
                    dst_ref=halo_recv.at[number, way],
                    send_sem=send_sem.at[first + way],
                    recv_sem=recv_sem.at[first + way],
                    device_id={"space": lax.rem(me + step, slabs)},
                    device_id_type=pl.DeviceIdType.MESH,
                )
            )
        up, down = copies

        @pl.when(me < slabs - 1)
        def _():
            up.start()

        @pl.when(me > 0)
        def _():
            down.start()

        return up, down

    def wait_halo(copies):
        up, down = copies

        @pl.when(me < slabs - 1)
        def _():
            up.wait_send()
            down.wait_recv()

        @pl.when(me > 0)
        def _():
            down.wait_send()
            up.wait_recv()

    needed = [set() for _ in range(modes)]
    for i in range(modes):
        for k, j, _ in links[i]:
            needed[j].add(k)

    def rest_terms(vec, number):
        for q in range(0, modes, 4):
            batch = range(q, min(modes, q + 4))
            values = [vec[m] for m in batch]
            sides = []
            for m, value in zip(batch, values):
                p, spot = divmod(m, width)
                above = roll(halo_recv[number, 1, p], width - 1 - spot)
                below = roll(halo_recv[number, 0, p], -spot)
                sides.append([
                    roll(value, -width), roll(value, width), roll(value, -1, 0), roll(value, 1, 0),
                    jnp.where(high_edge, above, roll(value, -1)),
                    jnp.where(low_edge, below, roll(value, 1)),
                ])
            results = {}
            for k in range(fields):
                factor = [coefs[k, n] for n in range(7)]
                for m, value, beside in zip(batch, values, sides):
                    if k == 0:
                        results[k, m] = -(
                            (factor[3] * beside[2] + factor[4] * beside[3])
                            + (factor[5] * beside[4] + factor[6] * beside[5])
                        )
                    elif k in needed[m]:
                        parts = [factor[1 + face] * beside[face] for face in range(6)]
                        results[k, m] = factor[0] * value - (
                            (parts[0] + parts[1]) + (parts[2] + parts[3]) + (parts[4] + parts[5])
                        )
            for (k, m), result in results.items():
                terms[k, m] = result

    def coupled(i):
        total = terms[0, i]
        by_weight = {}
        for k, j, weight in links[i]:
            by_weight.setdefault(weight, []).append((k, j))
        for weight, pairs in by_weight.items():
            part = terms[pairs[0][0], pairs[0][1]]
            for k, j in pairs[1:]:
                part = part + terms[k, j]
            total = total + (part if weight == 1.0 else np.float32(weight) * part)
        return total

    fit = zero
    for (low, high), copies in zip(halves, r_copies):
        for copy in copies:
            copy.wait()
        for q in range(low, high, 4):
            batch = range(q, min(high, q + 4))
            values = [[r_recv[b, p] for b in range(slabs)] for p in batch]
            residuals = [unpack(group, j) for group in values for j in range(slabs)]
            results = [line_inverse(residual) for residual in residuals]
            for n, (residual, smoothed) in enumerate(zip(residuals, results)):
                z_vec[q * slabs + n] = smoothed
                fit = fit + residual * smoothed
    copies = send_halo(z_vec, 0)
    first = 2 * (slabs - 1) + 4
    zx_recv[me] = pack_all(lambda m: z_vec[m], zx_send, 0, groups)
    zx_copies = exchange(zx_send, zx_recv, first)
    for copy in zx_copies:
        copy.start()
    wait_halo(copies)
    rest_terms(z_vec, 0)
    cross = square = zero
    for q in range(0, modes, 8):
        batch = range(q, min(modes, q + 8))
        rests = [coupled(i) for i in batch]
        results = [line_inverse(rest) for rest in rests]
        for i, rest, smoothed in zip(batch, rests, results):
            u_vec[i] = smoothed
            cross = cross + z_vec[i] * rest
            square = square + rest * smoothed
    copies = send_halo(u_vec, 1)
    first += slabs - 1
    ux_recv[me] = pack_all(lambda m: u_vec[m], ux_send, 0, groups)
    ux_copies = exchange(ux_send, ux_recv, first)
    for copy in ux_copies:
        copy.start()
    wait_halo(copies)
    rest_terms(u_vec, 1)
    last = [zero] * 4
    for i in range(modes):
        last[i % 4] = last[i % 4] + u_vec[i] * coupled(i)
    last = (last[0] + last[1]) + (last[2] + last[3])

    sums = zero
    for number, value in enumerate((fit, cross, square, last)):
        sums = jnp.where(row == number, jnp.sum(value, axis=0, keepdims=True), sums)
    sum_send[...] = sums
    first += slabs - 1
    sum_copies = []
    for n, (sample, slab) in enumerate(peers):
        sum_copies.append(
            pltpu.make_async_remote_copy(
                src_ref=sum_send,
                dst_ref=sum_recv.at[mine, me],
                send_sem=send_sem.at[first + n],
                recv_sem=recv_sem.at[first + n],
                device_id={"sample": sample, "space": slab},
                device_id_type=pl.DeviceIdType.MESH,
            )
        )
    for copy in sum_copies:
        copy.start()
    sum_recv[mine, me] = sums

    for copy in zx_copies:
        copy.wait()
    unpack_all(zx_recv, zx_vec)
    for copy in ux_copies:
        copy.wait()
    p, j = divmod(mean_mode, slabs)
    mean_send[0] = zx_vec[mean_mode]
    mean_send[1] = unpack([ux_recv[b, p] for b in range(slabs)], j)
    first += len(peers)
    mean_copies = []
    for away in range(1, samples):
        mean_copies.append(
            pltpu.make_async_remote_copy(
                src_ref=mean_send,
                dst_ref=mean_recv.at[mine],
                send_sem=send_sem.at[first + away - 1],
                recv_sem=recv_sem.at[first + away - 1],
                device_id={"sample": lax.rem(mine + away, samples)},
                device_id_type=pl.DeviceIdType.MESH,
            )
        )
    for copy in mean_copies:
        copy.start()
    mean_recv[mine] = mean_send[...]
    unpack_all(ux_recv, ux_vec)
    for copy in sum_copies[:slabs - 1]:
        copy.wait()

    def parts(sample):
        total = reduce(jnp.add, [sum_recv[sample, b] for b in range(slabs)])
        total = jnp.sum(total, axis=1, keepdims=True)
        f, e, g, h = (jnp.broadcast_to(total[n:n + 1], zero.shape) for n in range(4))
        curve = f + e
        step = f / curve
        ratio = (f * g - e * e) / (curve * curve)
        z_part = e / curve + ratio
        curve_next = (
            z_part * z_part * curve - 2.0 * z_part * step * (e + g) + step * step * (g + h)
        )
        step_next = ratio * f / curve_next
        return step + step_next * z_part, -step_next * step

    z_part, u_part = parts(mine)
    stores = []
    for q in range(0, modes, 8):
        batch = range(q, min(modes, q + 8))
        places = [idx_ref[modes + i] for i in batch]
        results = [z_part * zx_vec[place] + u_part * ux_vec[place] for place in places]
        for i, result in zip(batch, results):
            src_ref[i] = result
        rows_now = pl.ds(q, len(batch))
        stores.append(
            pltpu.make_async_copy(
                src_ref.at[rows_now], out_ref.at[rows_now], load_sem.at[2 + q // 8]
            )
        )
        stores[-1].start()
    for copy in sum_copies[slabs - 1:] + mean_copies:
        copy.wait()
    total = zero
    for sample in range(samples):
        z_part, u_part = parts(sample)
        total = total + (z_part * mean_recv[sample, 0] + u_part * mean_recv[sample, 1])
    total = total * (1.0 / samples)
    share = CELL_ROWS // samples
    result = total[0:share]
    for b in range(1, samples):
        result = jnp.where(mine == b, total[b * share:(b + 1) * share], result)
    grad_ref[...] = result
    for store in stores:
        store.wait()


def fused_on_device(adjoint_source, kl_bank, multi_index, sample_ids):
    slabs, samples = lax.axis_size("space"), lax.axis_size("sample")
    modes, variables = multi_index.shape
    fields = variables + 1
    code = reduce(lambda c, k: c * (DEGREE + 1) + multi_index[:, k], range(variables), 0)
    numbers = jnp.arange(modes, dtype=jnp.int32)
    rank = jnp.sum((code[None, :] < code[:, None]).astype(jnp.int32), axis=1)
    source = jnp.sum(jnp.where(rank[None, :] == numbers[:, None], numbers[None, :], 0), axis=1)
    index = jnp.concatenate([source, rank])
    tile = (CELL_ROWS, LANES)
    groups = modes // slabs
    f_groups = 2
    halos = -(-modes // (LANES // slabs))
    vmem = lambda *shape: pltpu.VMEM(shape + tile, jnp.float32)
    sems = 6 * (slabs - 1) + 4 + slabs * samples - 1 + samples - 1
    in_vmem = pl.BlockSpec(memory_space=pltpu.VMEM)
    in_hbm = pl.BlockSpec(memory_space=pltpu.HBM)
    in_smem = pl.BlockSpec(memory_space=pltpu.SMEM)
    state, gradient = pl.pallas_call(
        functools.partial(kernel, slabs, samples, variables),
        out_shape=(
            jax.ShapeDtypeStruct((modes,) + tile, jnp.float32),
            jax.ShapeDtypeStruct((CELL_ROWS // samples, LANES), jnp.float32),
        ),
        in_specs=[in_smem, in_smem, in_hbm, in_hbm],
        out_specs=(in_hbm, in_vmem),
        scratch_shapes=[
            vmem(modes), vmem(*kl_bank.shape[:2]),
            vmem(slabs, f_groups), vmem(slabs, f_groups),
            vmem(slabs, groups), vmem(slabs, groups),
            vmem(slabs, groups), vmem(slabs, groups),
            vmem(slabs, groups), vmem(slabs, groups),
            vmem(2, 2, halos), vmem(2, 2, halos),
            vmem(), vmem(samples, slabs), vmem(2), vmem(samples, 2),
            vmem(fields, 7), vmem(modes), vmem(modes), vmem(fields, modes),
            vmem(modes), vmem(modes),
            pltpu.SemaphoreType.DMA((sems,)), pltpu.SemaphoreType.DMA((sems,)),
            pltpu.SemaphoreType.DMA((2 + -(-modes // 8),)),
        ],
        compiler_params=pltpu.CompilerParams(
            collective_id=0, has_side_effects=True, vmem_limit_bytes=60 << 20
        ),
    )(
        sample_ids,
        index,
        adjoint_source.reshape((modes,) + tile),
        kl_bank.reshape(kl_bank.shape[:2] + tile),
    )
    return state.reshape(adjoint_source.shape), gradient[None]


def on_device(adjoint_source, kl_bank, multi_index, sample_ids):
    slabs, samples = lax.axis_size("space"), lax.axis_size("sample")
    modes, variables = multi_index.shape
    fits = (
        adjoint_source.shape == (1, modes, 1, CELL_ROWS, LANES)
        and slabs == 4
        and slabs < variables + 1 <= 2 * slabs - 2
        and CELL_ROWS % samples == 0
        and samples > 1
        and modes % slabs == 0
        and modes == len(basis_rows(variables))
    )
    work = fused_on_device if fits else plain_on_device
    return work(adjoint_source, kl_bank, multi_index, sample_ids)


def solution(mesh):
    return jax.shard_map(
        on_device,
        mesh=mesh,
        in_specs=(
            P(("groups", "sample"), None, "space", None, None),
            P(None, None, "space", None, None),
            P(),
            P(("groups", "sample")),
        ),
        out_specs=(
            P(("groups", "sample"), None, "space", None, None),
            P(("groups", "space"), "sample", None),
        ),
        check_vma=False,
    )
```
